128 devices in a mesh: dp: 32 (over x, y, core), mp: 4 (over z).
Axes of the slice: x: 4, y: 4, z: 4, core: 2. Of those that a mesh axis runs over, the one named last changes fastest.
Arguments:
- features: bfloat16 [18432, 8192], P('dp', 'mp'), may hold values from -6 to 6
- key_weight: bfloat16 [8192, 1024], P(None, 'mp'), may hold values from -0.0625 to 0.0625
- value_weight: bfloat16 [8192, 1024], P(None, 'mp'), may hold values from -0.0625 to 0.0625
- key_gain: float32 [128], replicated, may hold values from 0.1 to 1.9
- queries: bfloat16 [8192, 8192], P('dp', 'mp'), may hold values from -400 to 400
- grad_out: bfloat16 [8192, 8192], P('dp', 'mp'), may hold values from -6 to 6
- tile_dest: int32 [768, 1], replicated, may hold values from 0 to 31; in each aligned block of 24 rows (0 to 23, 24 to 47, ...) at most 2 rows name the same one
Outputs:
- attn_out: bfloat16 [8192, 8192], P('dp', 'mp')
- grad_queries: bfloat16 [8192, 8192], P('dp', 'mp')
- grad_features: bfloat16 [18432, 8192], P('dp', 'mp')
- grad_key_weight: float32 [8192, 1024], P(('mp', 'dp'))
- grad_value_weight: float32 [8192, 1024], P(('mp', 'dp'))
- grad_key_gain: float32 [128], replicated
The draws below stay inside these ranges and needn't reach their ends.
Inputs may be any that keep to these rules, and one draw needn't show every extreme that they name: Tile t, held by dp index t // 24, is read by text sample tile_dest[t, 0]; the tiles of one dp index name one sample at most 2 times, and every sample is named by some tile.
All inputs are finite; a program needn't handle non-finite values.
Results may differ from the reference program's by a relative error of at most 0.03105.
The reference program's roundings to bfloat16 on the way count: a program that leaves them out, or rounds other values in their place, can miss the bound.
Values may be sent and summed in bfloat16 or wider, within the bound.
No kernel may reach another device: no remote copies, remote signals or barrier semaphores. Data moves between devices by JAX's collectives and lax.ppermute only.
A program may use at most 192 MiB of HBM per device.

```python
import math
import jax
import jax.numpy as jnp
import numpy as np
from jax import lax

VW = 8192
HEADS = 64
KV_HEADS = 8
HD = 128
TOK_DEV = 256
TILE_DEV = 24
PATCH = 24
CAP = 2
NT = 768
TOKENS = 8192
N_DP = 32


def draw_queries(key, part):
    key = jax.random.fold_in(key, 11)
    values = jax.random.normal(key, (TOKENS, HEADS * HD), jnp.float32)
    values = jnp.clip(values, -6.0, 6.0)
    return values.astype(jnp.bfloat16)


def block_scale(key, dims, cuts, smallest, top_value):
    level = 1.0
    for axis_at, blocks in cuts:
        steps = jax.random.uniform(jax.random.fold_in(jax.random.fold_in(key, 6), axis_at), (blocks,), jnp.float32, smallest / len(cuts), top_value / len(cuts))
        level = level * jnp.repeat(jnp.exp(steps), dims[axis_at] // blocks).reshape((-1,) + (1,) * (len(dims) - 1 - axis_at))
    return level


def deal_out(stream_key, own, number, rows, count, top, limit, lean):
    sequence = jax.random.permutation(stream_key, count)
    heavy_load, usual = shares(count, rows * top, limit, lean, True), shares(count, rows * top, limit, lean, False)
    places = jnp.arange(count)

    def named(tallies, turn):
        used = int((tallies > 0).sum())
        fixed = max(1, used // 4)
        passed = fixed + (places - fixed + turn * (used - fixed)) % max(1, count - fixed)
        return jnp.zeros((count,), jnp.int32).at[sequence[jnp.where(places < fixed, places, passed)]].set(jnp.asarray(tallies, jnp.int32))

    tallies = jnp.where(number % 4 == 0, named(heavy_load, number // 4), named(usual, number - number // 4 - 1))
    mixed = jax.random.permutation(jax.random.fold_in(own, 3), count)
    source_of, receiver = mixed[0:count // 2 * 2:2], mixed[1:count // 2 * 2:2]
    margin = jnp.minimum(tallies[source_of] - 1, limit - tallies[receiver]) // 2
    margin = jnp.where((source_of == sequence[0]) | (receiver == sequence[0]) | (tallies[receiver] == 0), 0, jnp.maximum(margin, 0))
    passed = jax.random.randint(jax.random.fold_in(own, 4), (count // 2,), 0, 1 << 20) % (margin + 1)
    tallies = tallies.at[source_of].add(-passed).at[receiver].add(passed)
    labels = jnp.searchsorted(jnp.cumsum(tallies), jnp.arange(rows * top), side="right").astype(jnp.int32)
    table = labels.reshape(top, rows).T
    table = table[jax.random.permutation(jax.random.fold_in(own, 1), rows)]
    turn = jax.random.randint(jax.random.fold_in(own, 2), (rows, 1), 0, top)
    return jnp.take_along_axis(table, (jnp.arange(top)[None, :] + turn) % top, axis=1)


def shares(amount, total, reach, skew, full):
    weights = [(1 << 20) // math.isqrt(grade ** skew) + 1 for grade in range(1, amount + 1)]
    largest = reach if full else min(reach, max(-(-total // amount), total * weights[0] // sum(weights)))
    least = 1 if total - largest >= amount - 1 else 0
    holding, surplus = [largest] + [least] * (amount - 1), total - largest - least * (amount - 1)
    while surplus > 0:
        free = [i for i in range(1, amount) if holding[i] < largest] or [i for i in range(1, amount) if holding[i] < reach]
        mass, remaining = sum([weights[i] for i in free]), surplus
        for i in free:
            more = min(reach - holding[i], max(1, remaining * weights[i] // mass), surplus)
            holding[i] = holding[i] + more
            surplus = surplus - more
    return np.array(holding)


def gaussian(stream_key, extent, spread, reach, pieces=(), kind=jnp.bfloat16):
    loudness = block_scale(stream_key, extent, pieces, -0.22, 0.18) if pieces else 1.0
    drawn = jax.random.normal(stream_key, extent, jnp.float32) * spread * loudness
    return jnp.minimum(jnp.maximum(drawn, -reach), reach).astype(kind)


def setup_inputs(seed: int = 0) -> dict:
    arg_keys = jax.random.split(jax.random.key(seed), 8)
    features = gaussian(arg_keys[0], (NT * PATCH, VW), 1.0, 6.0, ((0, 32), (1, 4)))
    key_weight = gaussian(arg_keys[1], (VW, KV_HEADS * HD), VW ** -0.5, 0.0625, ((1, 4),))
    value_weight = gaussian(arg_keys[2], (VW, KV_HEADS * HD), VW ** -0.5, 0.0625, ((1, 4),))
    key_gain = jnp.clip(1.0 + 0.18 * jax.random.normal(arg_keys[3], (HD,), jnp.float32), 0.1, 1.9)
    queries = draw_queries(jax.random.fold_in(arg_keys[7], 71), 0)
    grad_out = gaussian(arg_keys[5], (TOKENS, HEADS * HD), 1.0, 6.0, ((0, 32), (1, 4)))
    tile_dest_keys = jax.random.split(jax.random.fold_in(arg_keys[6], 1), NT // TILE_DEV)
    tile_dest_turns = jax.random.permutation(jax.random.fold_in(arg_keys[6], 3), NT // TILE_DEV)
    tile_dest = jax.vmap(lambda own, number: deal_out(jax.random.fold_in(arg_keys[6], 2), own, number, TILE_DEV, N_DP, 1, CAP, 2))(tile_dest_keys, tile_dest_turns).reshape((NT, 1))
    return {"features": features, "key_weight": key_weight, "value_weight": value_weight, "key_gain": key_gain, "queries": queries, "grad_out": grad_out, "tile_dest": tile_dest}


EPSILON = 1e-05

def head_pass(query_rows, key_rows, value_rows, grad_rows, live_keys, score_scale):
    scores = jnp.dot(query_rows, key_rows.T, preferred_element_type=jnp.float32) * score_scale
    scores = jnp.where(live_keys[None, :], scores, -1e+30)
    row_max = lax.optimization_barrier(jnp.max(scores, axis=1, keepdims=True))
    weights = jnp.exp(scores - row_max)
    attn_probs = weights / lax.optimization_barrier(jnp.sum(weights, axis=1, keepdims=True))
    probs_low = attn_probs.astype(jnp.bfloat16)
    attn_sum = jnp.dot(probs_low, value_rows, preferred_element_type=jnp.float32)
    grad_probs = jnp.dot(grad_rows, value_rows.T, preferred_element_type=jnp.float32)
    row_delta = lax.optimization_barrier(jnp.sum(grad_rows.astype(jnp.float32) * attn_sum, axis=1, keepdims=True))
    grad_scores = (attn_probs * (grad_probs - row_delta)).astype(jnp.bfloat16)
    grad_query = jnp.dot(grad_scores, key_rows, preferred_element_type=jnp.float32) * score_scale
    grad_keys = jnp.dot(grad_scores.T, query_rows, preferred_element_type=jnp.float32) * score_scale
    grad_values = jnp.dot(probs_low.T, grad_rows, preferred_element_type=jnp.float32)
    return (attn_sum.astype(jnp.bfloat16), grad_query.astype(jnp.bfloat16), grad_keys, grad_values)

def attend(queries, grad_out, key_rows, value_rows, live_keys, head_dim):
    tokens_here = queries.shape[0]
    kv_local = key_rows.shape[1] // head_dim
    heads_per_kv = queries.shape[1] // (kv_local * head_dim)
    score_scale = head_dim ** (-0.5)
    query_heads = queries.reshape(tokens_here, kv_local, heads_per_kv, head_dim).transpose(1, 2, 0, 3)
    grad_heads = grad_out.reshape(tokens_here, kv_local, heads_per_kv, head_dim).transpose(1, 2, 0, 3)
    key_heads = key_rows.reshape(-1, kv_local, head_dim).transpose(1, 0, 2)
    value_heads = value_rows.reshape(-1, kv_local, head_dim).transpose(1, 0, 2)

    def per_kv_head(operands):
        group_queries, group_grads, group_keys, group_values = operands

        def step(totals, head_inputs):
            out_head, grad_query, grad_keys, grad_values = head_pass(head_inputs[0], group_keys, group_values, head_inputs[1], live_keys, score_scale)
            return ((totals[0] + grad_keys, totals[1] + grad_values), (out_head, grad_query))
        zero_grads = jnp.zeros(group_keys.shape, jnp.float32)
        grad_sums, stacked = lax.scan(step, (zero_grads, zero_grads), (group_queries, group_grads))
        return (stacked[0], stacked[1], grad_sums[0], grad_sums[1])
    out_heads, query_grads, key_grads, value_grads = lax.map(per_kv_head, (query_heads, grad_heads, key_heads, value_heads))
    attn_out = out_heads.transpose(2, 0, 1, 3).reshape(tokens_here, -1)
    grad_queries = query_grads.transpose(2, 0, 1, 3).reshape(tokens_here, -1)
    key_grad_rows = key_grads.transpose(1, 0, 2).reshape(-1, kv_local * head_dim).astype(jnp.bfloat16)
    value_grad_rows = value_grads.transpose(1, 0, 2).reshape(-1, kv_local * head_dim).astype(jnp.bfloat16)
    return (attn_out, grad_queries, key_grad_rows, value_grad_rows)

def normalize_keys(key_pre, key_gain):
    inverse_rms = lax.rsqrt(lax.optimization_barrier(jnp.mean(key_pre * key_pre, axis=-1, keepdims=True)) + EPSILON)
    return (key_pre * inverse_rms * key_gain, inverse_rms)

def norm_backward(key_pre, inverse_rms, key_gain, grad_normed):
    gain_terms = lax.optimization_barrier(jnp.sum(grad_normed * key_pre * inverse_rms, axis=(0, 1)))
    scaled = key_gain * grad_normed
    grad_pre = inverse_rms * (scaled - key_pre * inverse_rms * inverse_rms * lax.optimization_barrier(jnp.mean(scaled * key_pre, axis=-1, keepdims=True)))
    return (grad_pre, gain_terms)

def slot_ranks(readers, sources, per_source):
    by_source = readers.reshape(sources, per_source)
    same_reader = by_source[:, :, None] == by_source[:, None, :]
    positions = jnp.arange(per_source, dtype=jnp.int32)
    before = positions[None, :] < positions[:, None]
    return lax.optimization_barrier(jnp.sum(jnp.where(same_reader & before[None], 1, 0), axis=2)).astype(jnp.int32)

def reference(features, key_weight, value_weight, key_gain, queries, grad_out, tile_dest):
    row_count = features.shape[0]
    width = KV_HEADS * HD
    readers = tile_dest[:, 0]
    tile_count = readers.shape[0]
    ranks = slot_ranks(readers, N_DP, TILE_DEV).reshape(-1)
    owners = jnp.arange(tile_count, dtype=jnp.int32) // TILE_DEV
    slot_ids = (owners * CAP + ranks).astype(jnp.int32)
    table = jnp.full((N_DP, N_DP * CAP), -1, jnp.int32).at[readers, slot_ids].set(jnp.arange(tile_count, dtype=jnp.int32))
    key_pre = jnp.dot(features, key_weight, preferred_element_type=jnp.float32).reshape(row_count, KV_HEADS, HD)
    normed, inverse_rms = normalize_keys(key_pre, key_gain)
    key_tiles = normed.astype(jnp.bfloat16).reshape(tile_count, PATCH, width)
    value_tiles = jnp.dot(features, value_weight, preferred_element_type=jnp.float32).astype(jnp.bfloat16).reshape(tile_count, PATCH, width)
    sample_queries = queries.reshape(N_DP, TOK_DEV, HEADS * HD)
    sample_grads = grad_out.reshape(N_DP, TOK_DEV, HEADS * HD)

    def per_sample(totals, inputs):
        slot_tiles, sample_query, sample_grad = inputs
        live_slots = slot_tiles >= 0
        tile_index = jnp.maximum(slot_tiles, 0).astype(jnp.int32)
        key_rows = jnp.take(key_tiles, tile_index, axis=0).reshape(-1, width)
        value_rows = jnp.take(value_tiles, tile_index, axis=0).reshape(-1, width)
        live_keys = jnp.broadcast_to(live_slots[:, None], (live_slots.shape[0], PATCH)).reshape(-1)
        attn_out, grad_queries, key_grad_rows, value_grad_rows = attend(sample_query, sample_grad, key_rows, value_rows, live_keys, HD)
        target = jnp.where(live_slots, slot_tiles, tile_count).astype(jnp.int32)
        key_grads = totals[0].at[target].set(key_grad_rows.reshape(-1, PATCH, width), mode='drop')
        value_grads = totals[1].at[target].set(value_grad_rows.reshape(-1, PATCH, width), mode='drop')
        return ((key_grads, value_grads), (attn_out, grad_queries))
    empty = jnp.zeros((tile_count, PATCH, width), jnp.bfloat16)
    grads, outputs = lax.scan(per_sample, (empty, empty), (table, sample_queries, sample_grads))
    key_grad = grads[0].reshape(row_count, KV_HEADS, HD).astype(jnp.float32)
    value_grad = grads[1].reshape(row_count, width)
    grad_pre, gain_terms = norm_backward(key_pre, inverse_rms, key_gain, key_grad)
    grad_pre_low = grad_pre.astype(jnp.bfloat16).reshape(row_count, width)
    grad_key_weight = jnp.dot(features.T, grad_pre_low, preferred_element_type=jnp.float32)
    grad_value_weight = jnp.dot(features.T, value_grad, preferred_element_type=jnp.float32)
    grad_features = (jnp.dot(grad_pre_low, key_weight.T, preferred_element_type=jnp.float32) + jnp.dot(value_grad, value_weight.T, preferred_element_type=jnp.float32)).astype(jnp.bfloat16)
    attn_out = outputs[0].reshape(TOKENS, HEADS * HD)
    grad_queries = outputs[1].reshape(TOKENS, HEADS * HD)
    return (attn_out, grad_queries, grad_features, grad_key_weight, grad_value_weight, gain_terms)
```

```python
import functools
import jax
import jax.numpy as jnp
from jax import lax
from jax.experimental import pallas as pl
from jax.experimental.pallas import tpu as pltpu
from jax.sharding import PartitionSpec as P

EPSILON = 1e-05
BF16 = jnp.bfloat16
F32 = jnp.float32
LOG2E = 1.4426950408889634
NT_DIMS = (((1,), (1,)), ((), ()))


def dot(left, right):
    return jnp.dot(left, right, preferred_element_type=F32)


def dot_nt(left, right):
    return lax.dot_general(left, right, NT_DIMS, preferred_element_type=F32)


def attend_kernel(scale, last, q_ref, g_ref, kv_ref, bias_ref, *refs):
    o_ref, gq_ref, gkv_ref, kaug, kt, vt, gk_sum, gv_sum = refs[-8:]
    head = pl.program_id(0)
    hd = q_ref.shape[1]

    @pl.when(head == 0)
    def _():
        kaug[:, :hd] = kv_ref[:, :hd]
        kaug[:, hd:] = bias_ref[...]
        kt[...] = kv_ref[:, :hd].T
        vt[...] = kv_ref[:, hd:].T
        gk_sum[...] = jnp.zeros_like(gk_sum)
        gv_sum[...] = jnp.zeros_like(gv_sum)

    q = q_ref[...]
    g = g_ref[...]
    lanes = lax.broadcasted_iota(jnp.int32, q.shape, 1)
    ones = jnp.where(lanes == 0, 1.0, 0.0).astype(BF16)
    scores = dot_nt(kaug[...], jnp.concatenate([q, ones], axis=1))
    top = jnp.max(scores, axis=0, keepdims=True)
    weights = jnp.exp2((scores - top) * (scale * LOG2E))
    probs = weights * (1.0 / jnp.sum(weights, axis=0, keepdims=True))
    low = probs.astype(BF16)
    out_t = dot(vt[...], low)
    grad_probs = dot_nt(kv_ref[:, hd:], g)
    delta = jnp.sum(g.astype(F32).T * out_t, axis=0, keepdims=True)
    grad_scores = (probs * (grad_probs - delta)).astype(BF16)
    gq_t = dot(kt[...], grad_scores) * scale
    o_ref[...] = out_t.T.astype(BF16)
    gq_ref[...] = gq_t.T.astype(BF16)
    gk_sum[...] += dot(grad_scores, q)
    gv_sum[...] += dot(low, g)

    @pl.when(head == last)
    def _():
        gkv_ref[:, :hd] = (gk_sum[...] * scale).astype(BF16)
        gkv_ref[:, hd:] = gv_sum[...].astype(BF16)


def attend(queries, grad_out, kv, bias, group, groups, hd, so_far):
    tokens, width = queries.shape
    heads = width // hd // groups
    keys = kv.shape[0]
    by_head = pl.BlockSpec((tokens, hd), lambda h: (0, group * heads + h))
    whole = lambda a: pl.BlockSpec(a.shape, lambda h: (0, 0))
    extra = [] if so_far is None else list(so_far)
    out = jax.ShapeDtypeStruct((tokens, width), BF16)
    return pl.pallas_call(
        functools.partial(attend_kernel, hd**-0.5, heads - 1),
        grid=(heads,),
        in_specs=[by_head, by_head, whole(kv), whole(bias)]
        + [pl.BlockSpec(memory_space=pl.ANY)] * len(extra),
        out_specs=[by_head, by_head, whole(kv)],
        out_shape=[out, out, jax.ShapeDtypeStruct(kv.shape, BF16)],
        scratch_shapes=[
            pltpu.VMEM((keys, 2 * hd), BF16),
            pltpu.VMEM((hd, keys), BF16),
            pltpu.VMEM((hd, keys), BF16),
            pltpu.VMEM((keys, hd), F32),
            pltpu.VMEM((keys, hd), F32),
        ],
        input_output_aliases={} if not extra else {4: 0, 5: 1},
        compiler_params=pltpu.CompilerParams(
            dimension_semantics=("arbitrary",), vmem_limit_bytes=48 * 2**20
        ),
        cost_estimate=pl.CostEstimate(
            flops=12 * heads * tokens * keys * hd,
            bytes_accessed=8 * heads * tokens * hd + 8 * keys * hd,
            transcendentals=heads * tokens * keys,
        ),
        name="attend",
    )(queries, grad_out, kv, bias, *extra)


def weight_grad_kernel(mine_ref, theirs_ref, g_ref, other_ref, out_ref):
    total = dot(mine_ref[...], g_ref[...]) + dot(theirs_ref[...], other_ref[...])
    out_ref[...] = total.astype(out_ref.dtype)


def weight_grad(mine, theirs, grads, other_grads, tile):
    rows, depth = mine.shape
    cols = grads.shape[1]
    return pl.pallas_call(
        weight_grad_kernel,
        grid=(cols // tile,),
        in_specs=[pl.BlockSpec((rows, depth), lambda i: (0, 0))] * 2
        + [pl.BlockSpec((depth, tile), lambda i: (0, i))] * 2,
        out_specs=pl.BlockSpec((rows, tile), lambda i: (0, i)),
        out_shape=jax.ShapeDtypeStruct((rows, cols), BF16),
        compiler_params=pltpu.CompilerParams(
            dimension_semantics=("arbitrary",), vmem_limit_bytes=40 * 2**20
        ),
        cost_estimate=pl.CostEstimate(
            flops=4 * rows * depth * cols,
            bytes_accessed=4 * rows * depth + 4 * depth * cols + 2 * rows * cols,
            transcendentals=0,
        ),
        name="weight_grad",
    )(mine, theirs, grads, other_grads)


def slot_ranks(readers, sources, per_source):
    by_source = readers.reshape(sources, per_source)
    same_reader = by_source[:, :, None] == by_source[:, None, :]
    positions = jnp.arange(per_source, dtype=jnp.int32)
    before = positions[None, :] < positions[:, None]
    return jnp.sum(jnp.where(same_reader & before[None], 1, 0), axis=2).astype(jnp.int32)


def body(sizes, features, key_weight, value_weight, key_gain, queries, grad_out, tile_dest):
    nx, ny, nc, nz = sizes
    n_dp = nx * ny * nc
    dp, z = lax.axis_index("dp"), lax.axis_index("mp")
    core = lax.rem(dp, nc)
    py = lax.rem(dp // nc, ny)
    px = dp // (nc * ny)
    hd = key_gain.shape[0]
    rows, depth = features.shape
    width = key_weight.shape[1]
    groups = width // hd

    def z_shift(a, d):
        return lax.ppermute(a, "mp", [(i, (i + d) % nz) for i in range(nz)])

    def moved(a, dx, dy, flip=0):
        perm = []
        for i in range(n_dp):
            x, y, c = i // (ny * nc), i // nc % ny, i % nc
            perm.append((i, (((x + dx) % nx) * ny + (y + dy) % ny) * nc + (c ^ flip)))
        return lax.ppermute(a, "dp", perm)

    def swap(a):
        return moved(a, 0, 0, 1)

    def piece(weight, d, start, count):
        return lax.dynamic_slice_in_dim(weight, lax.rem(z + d, nz) * depth + start, count)

    half = depth // nc
    share = depth // n_dp
    value_piece = [z_shift(piece(value_weight, d, dp * share, share), d) for d in range(1, nz)]
    value_piece = jnp.concatenate([piece(value_weight, 0, dp * share, share)] + value_piece, axis=1)
    value_rows_w = lax.all_gather(value_piece, "dp", axis=0, tiled=True)

    key_blocks = [piece(key_weight, 0, 0, depth)]
    for d in range(1, nz):
        got = z_shift(piece(key_weight, d, core * half, half), d)
        other = swap(got)
        key_blocks.append(
            jnp.where(
                core == 0,
                jnp.concatenate([got, other], axis=0),
                jnp.concatenate([other, got], axis=0),
            )
        )
    key_rows_w = jnp.concatenate(key_blocks, axis=1)

    by_core = features.T.reshape(nx * ny, nc, share, rows)
    mine = lax.dynamic_index_in_dim(by_core, core, 1, keepdims=False).reshape(-1, rows)
    given = lax.dynamic_index_in_dim(by_core, 1 - core, 1, keepdims=False).reshape(-1, rows)
    theirs = swap(given)

    readers = tile_dest[:, 0]
    per_source = readers.shape[0] // n_dp
    patch = rows // per_source
    capacity = max(2, (2 * per_source + n_dp - 1) // n_dp)
    ranks = slot_ranks(readers, n_dp, per_source)
    my_readers = lax.dynamic_slice_in_dim(readers, dp * per_source, per_source)
    my_ranks = lax.dynamic_index_in_dim(ranks, dp, 0, keepdims=False)
    send_slot = my_readers * capacity + my_ranks
    slots = n_dp * capacity
    fills = send_slot[None, :] == jnp.arange(slots, dtype=jnp.int32)[:, None]
    slot_source = jnp.min(
        jnp.where(fills, jnp.arange(per_source, dtype=jnp.int32)[None, :], per_source), axis=1
    )
    counts = jnp.sum(jnp.where(readers.reshape(n_dp, per_source) == dp, 1, 0), axis=1)
    live_slots = jnp.arange(capacity, dtype=jnp.int32)[None, :] < counts[:, None]
    live = jnp.broadcast_to(live_slots[:, :, None], (n_dp, capacity, patch)).reshape(-1)
    bias = jnp.where(
        live[:, None] | (jnp.arange(hd) > 0)[None, :], jnp.float32(0), jnp.float32(-1e30)
    ).astype(BF16)

    key_parts = dot(features, key_rows_w)
    value_parts = dot(features, value_rows_w)

    def block(a, d):
        return a[:, d * width : (d + 1) * width]

    key_pre, value_sum = block(key_parts, 0), block(value_parts, 0)
    for d in range(1, nz):
        key_pre = key_pre + z_shift(block(key_parts, d), nz - d)
    for d in range(1, nz):
        value_sum = value_sum + z_shift(block(value_parts, d).astype(BF16), nz - d).astype(F32)
    key_pre = key_pre.reshape(rows, groups, hd)
    inverse_rms = lax.rsqrt(jnp.mean(key_pre * key_pre, axis=-1, keepdims=True) + EPSILON)
    key_rows = (key_pre * inverse_rms * key_gain).astype(BF16)
    value_rows = value_sum.astype(BF16).reshape(rows, groups, hd)

    gain_terms = jnp.zeros((hd,), F32)
    outputs = None
    group_grads = []
    for j in range(groups):
        packed = jnp.concatenate([key_rows[:, j], value_rows[:, j]], axis=1)
        packed = packed.reshape(per_source, patch, 2 * hd)
        padded = jnp.concatenate([packed, jnp.zeros((1,) + packed.shape[1:], BF16)], axis=0)
        sent = jnp.take(padded, slot_source, axis=0).reshape(n_dp, capacity * patch, 2 * hd)
        arrived = lax.all_to_all(sent, "dp", split_axis=0, concat_axis=0, tiled=True)
        *outputs, returned = attend(
            queries, grad_out, arrived.reshape(-1, 2 * hd), bias, j, groups, hd, outputs
        )
        home = lax.all_to_all(
            returned.reshape(n_dp, capacity * patch, 2 * hd),
            "dp",
            split_axis=0,
            concat_axis=0,
            tiled=True,
        ).reshape(slots, patch, 2 * hd)
        tile_grads = jnp.take(home, send_slot, axis=0).reshape(rows, 2 * hd)
        key_grad = tile_grads[:, :hd].astype(F32)
        pre, inv = key_pre[:, j], inverse_rms[:, j]
        gain_terms = gain_terms + jnp.sum(key_grad * pre * inv, axis=0)
        scaled = key_gain * key_grad
        grad_pre = inv * (
            scaled - pre * inv * inv * jnp.mean(scaled * pre, axis=-1, keepdims=True)
        )
        mine_grads = jnp.concatenate([grad_pre.astype(BF16), tile_grads[:, hd:]], axis=1)
        group_grads.append([mine_grads] + [z_shift(mine_grads, d) for d in range(1, nz)])

    gain_all = lax.all_gather(gain_terms[None], "dp", axis=0, tiled=True)
    gain_z = lax.all_gather(jnp.sum(gain_all, axis=0)[None], "mp", axis=0, tiled=True)
    grad_key_gain = jnp.sum(gain_z, axis=0)

    key_g = jnp.concatenate([g[d][:, :hd] for d in range(nz) for g in group_grads], axis=1)
    value_g = jnp.concatenate([g[d][:, hd:] for d in range(nz) for g in group_grads], axis=1)
    grad_features = (dot_nt(key_g, key_rows_w) + dot_nt(value_g, value_rows_w)).astype(BF16)

    key_part = weight_grad(mine, theirs, key_g, swap(key_g), 512)
    value_part = weight_grad(mine, theirs, value_g, swap(value_g), 512)
    full = key_part.shape[1]
    key_part = key_part.reshape(nx, ny, share, full)
    value_part = value_part.reshape(nx, ny, share, full)

    def exchange(part, axis, place, count, step):
        take = lambda d: lax.dynamic_index_in_dim(
            part, lax.rem(place + d, count), axis, keepdims=False
        )
        total = take(0).astype(F32)
        for d in range(1, count):
            total = total + step(take(d), d).astype(F32)
        return total

    x_step = lambda a, d: moved(a, d, 0)
    y_step = lambda a, d: moved(a, 0, d)
    key_mid = exchange(key_part, 0, px, nx, x_step).astype(BF16)
    value_mid = exchange(value_part, 1, py, ny, y_step).astype(BF16)
    key_sum = exchange(key_mid, 0, py, ny, y_step)
    value_sum = exchange(value_mid, 0, px, nx, x_step)

    def in_order(a):
        blocks = a.reshape(share, nz, width)
        out = jnp.zeros_like(blocks)
        for d in range(nz):
            out = lax.dynamic_update_slice_in_dim(
                out, blocks[:, d : d + 1], lax.rem(z + nz - d, nz), 1
            )
        return out.reshape(share, nz * width)

    return (
        outputs[0],
        outputs[1],
        grad_features,
        in_order(key_sum),
        in_order(value_sum),
        grad_key_gain,
    )


def solution(mesh):
    n_dp, nz = mesh.shape["dp"], mesh.shape["mp"]
    nc = 2
    ny = 4
    sizes = (n_dp // (nc * ny), ny, nc, nz)
    in_specs = (P("dp", "mp"), P(None, "mp"), P(None, "mp"), P(), P("dp", "mp"), P("dp", "mp"), P())
    out_specs = (
        P("dp", "mp"),
        P("dp", "mp"),
        P("dp", "mp"),
        P(("mp", "dp"), None),
        P(("mp", "dp"), None),
        P(),
    )
    return jax.shard_map(
        functools.partial(body, sizes),
        mesh=mesh,
        in_specs=in_specs,
        out_specs=out_specs,
        check_vma=False,
    )
```

```python
import functools
import jax
import jax.numpy as jnp
from jax import lax
from jax.experimental import pallas as pl
from jax.experimental.pallas import tpu as pltpu
from jax.sharding import PartitionSpec as P

EPSILON = 1e-05
BF16 = jnp.bfloat16
F32 = jnp.float32
LOG2E = 1.4426950408889634
VMEM_BYTES = 56 * 2**20
NT_DIMS = (((1,), (1,)), ((), ()))


def after(a, *others):
    return lax.optimization_barrier((a, *others))[0]


def dot(left, right):
    return jnp.dot(left, right, preferred_element_type=F32)


def dot_nt(left, right):
    return lax.dot_general(left, right, NT_DIMS, preferred_element_type=F32)


STEP_HEADS = 4


def attend_kernel(scale, steps, first, q_hbm, g_hbm, kv_ref, bias_ref, *refs):
    o_ref, gq_ref, gkv_ref, kaug, kt, vt, gk_sum, gv_sum, q_all, g_all, sems = refs[-11:]
    step = pl.program_id(0)
    hd = kt.shape[0]
    size = q_all.shape[2]
    count = size // hd

    def load(n, at):
        cols = pl.ds((first + n) * size, size)
        return [
            pltpu.make_async_copy(q_hbm.at[:, cols], q_all.at[at], sems.at[0, at]),
            pltpu.make_async_copy(g_hbm.at[:, cols], g_all.at[at], sems.at[1, at]),
        ]

    @pl.when(step == 0)
    def _():
        for n in range(steps):
            for copy in load(n, n):
                copy.start()
        kaug[:, :hd] = kv_ref[:, :hd]
        kaug[:, hd:] = bias_ref[...]
        kt[...] = kv_ref[:, :hd].T
        vt[...] = kv_ref[:, hd:].T
        gk_sum[...] = jnp.zeros_like(gk_sum)
        gv_sum[...] = jnp.zeros_like(gv_sum)

    for copy in load(0, step):
        copy.wait()
    cols = [slice(i * hd, (i + 1) * hd) for i in range(count)]
    qs = [q_all[step, :, c] for c in cols]
    gs = [g_all[step, :, c] for c in cols]
    lanes = lax.broadcasted_iota(jnp.int32, qs[0].shape, 1)
    ones = jnp.where(lanes == 0, 1.0, 0.0).astype(BF16)
    scores = [dot_nt(kaug[...], jnp.concatenate([q, ones], axis=1)) for q in qs]
    grad_probs = [dot_nt(kv_ref[:, hd:], g) for g in gs]
    lows, grad_scores = [], []
    for i in range(count):
        top = jnp.max(scores[i], axis=0, keepdims=True)
        weights = jnp.exp2((scores[i] - top) * (scale * LOG2E))
        probs = weights * (1.0 / jnp.sum(weights, axis=0, keepdims=True))
        low = probs.astype(BF16)
        out_t = dot(vt[...], low)
        delta = jnp.sum(gs[i].astype(F32).T * out_t, axis=0, keepdims=True)
        grad_low = (probs * (grad_probs[i] - delta)).astype(BF16)
        gq_t = dot(kt[...], grad_low) * scale
        o_ref[:, cols[i]] = out_t.T.astype(BF16)
        gq_ref[:, cols[i]] = gq_t.T.astype(BF16)
        lows.append(low)
        grad_scores.append(grad_low)
    gk_sum[...] += dot(jnp.concatenate(grad_scores, axis=1), jnp.concatenate(qs, axis=0))
    gv_sum[...] += dot(jnp.concatenate(lows, axis=1), jnp.concatenate(gs, axis=0))

    @pl.when(step == steps - 1)
    def _():
        gkv_ref[:, :hd] = (gk_sum[...] * scale).astype(BF16)
        gkv_ref[:, hd:] = gv_sum[...].astype(BF16)


def attend(queries, grad_out, kv, bias, group, groups, hd, so_far):
    tokens, width = queries.shape
    heads = width // hd // groups
    steps = heads // STEP_HEADS
    keys = kv.shape[0]
    by_head = pl.BlockSpec((tokens, hd * STEP_HEADS), lambda h: (0, group * steps + h))
    whole = lambda a: pl.BlockSpec(a.shape, lambda h: (0, 0))
    extra = [] if so_far is None else list(so_far)
    out = jax.ShapeDtypeStruct((tokens, width), BF16)
    return pl.pallas_call(
        functools.partial(attend_kernel, hd**-0.5, steps, group * steps),
        grid=(steps,),
        in_specs=[pl.BlockSpec(memory_space=pltpu.HBM)] * 2
        + [whole(kv), whole(bias)]
        + [pl.BlockSpec(memory_space=pl.ANY)] * len(extra),
        out_specs=[by_head, by_head, whole(kv)],
        out_shape=[out, out, jax.ShapeDtypeStruct(kv.shape, BF16)],
        scratch_shapes=[
            pltpu.VMEM((keys, 2 * hd), BF16),
            pltpu.VMEM((hd, keys), BF16),
            pltpu.VMEM((hd, keys), BF16),
            pltpu.VMEM((keys, hd), F32),
            pltpu.VMEM((keys, hd), F32),
            pltpu.VMEM((steps, tokens, hd * STEP_HEADS), BF16),
            pltpu.VMEM((steps, tokens, hd * STEP_HEADS), BF16),
            pltpu.SemaphoreType.DMA((2, steps)),
        ],
        input_output_aliases={} if not extra else {4: 0, 5: 1},
        compiler_params=pltpu.CompilerParams(
            dimension_semantics=("arbitrary",), vmem_limit_bytes=VMEM_BYTES
        ),
        cost_estimate=pl.CostEstimate(
            flops=40 * heads * tokens * keys * hd,
            bytes_accessed=8 * heads * tokens * hd + 8 * keys * hd,
            transcendentals=heads * tokens * keys,
        ),
        name="attend",
    )(queries, grad_out, kv, bias, *extra)


def no_grid(kernel, in_specs, out_shape, scratch, flops, moved_bytes, name, first_out=None):
    vmem = pl.BlockSpec(memory_space=pltpu.VMEM)
    smem = pl.BlockSpec(memory_space=pltpu.SMEM)
    out_specs = [vmem] * len(out_shape)
    if first_out is not None:
        out_specs[0] = pl.BlockSpec(memory_space=first_out)
    return pl.pallas_call(
        kernel,
        in_specs=[smem if kind == "s" else vmem for kind in in_specs],
        out_specs=out_specs,
        out_shape=out_shape,
        scratch_shapes=scratch,
        compiler_params=pltpu.CompilerParams(vmem_limit_bytes=VMEM_BYTES),
        cost_estimate=pl.CostEstimate(
            flops=flops, bytes_accessed=moved_bytes, transcendentals=0
        ),
        name=name,
    )


def project_key_kernel(nz, at_ref, feature_ref, own_ref, *refs):
    got, other = refs[: nz - 1], refs[nz - 1 : 2 * nz - 2]
    kept, outs, weight, sem = refs[2 * nz - 2], refs[2 * nz - 1 : -2], refs[-2], refs[-1]
    wide = own_ref.shape[1]
    half = weight.shape[0] // 2
    weight[:, :wide] = own_ref[...]
    mine = pl.ds(pl.multiple_of(at_ref[0] * half, half), half)
    theirs = pl.ds(pl.multiple_of((1 - at_ref[0]) * half, half), half)
    for d in range(1, nz):
        cols = slice(d * wide, (d + 1) * wide)
        weight[mine, cols] = got[d - 1][...]
        weight[theirs, cols] = other[d - 1][...]
    keep = pltpu.make_async_copy(weight, kept, sem)
    keep.start()
    for d in range(nz):
        outs[d][...] = dot(feature_ref[...], weight[:, d * wide : (d + 1) * wide])
    keep.wait()


def project_key(where, features, own, got, other):
    rows, depth = features.shape
    wide = own.shape[1]
    nz = len(got) + 1
    out = [jax.ShapeDtypeStruct((depth, nz * wide), BF16)]
    out += [jax.ShapeDtypeStruct((rows, wide), F32)] * nz
    weight, *parts = no_grid(
        functools.partial(project_key_kernel, nz),
        "s" + "v" * (2 * nz),
        out,
        [pltpu.VMEM((depth, nz * wide), BF16), pltpu.SemaphoreType.DMA],
        4 * rows * depth * nz * wide,
        2 * rows * depth + 4 * depth * nz * wide + 4 * rows * nz * wide,
        "project_key",
        pltpu.HBM,
    )(where, features, own, *got, *other)
    return weight, parts


def project_value_kernel(nz, at_ref, feature_ref, *refs):
    ny = (len(refs) - nz - 3) // 2
    pieces, others = refs[:ny], refs[ny : 2 * ny]
    kept, outs, weight, sem = refs[2 * ny], refs[2 * ny + 1 : -2], refs[-2], refs[-1]
    size = pieces[0].shape[0]
    for e in range(ny):
        y = lax.rem(at_ref[1] + ny - e, ny)
        for core, src in ((at_ref[0], pieces[e]), (1 - at_ref[0], others[e])):
            start = pl.multiple_of((core * ny + y) * size, size)
            weight[pl.ds(start, size), :] = src[...]
    keep = pltpu.make_async_copy(weight, kept, sem)
    keep.start()
    wide = outs[0].shape[1]
    for d in range(nz):
        part = dot(feature_ref[...], weight[:, d * wide : (d + 1) * wide])
        outs[d][...] = part.astype(outs[d].dtype)
    keep.wait()


def project_value(where, features, pieces, others, nz):
    rows, depth = features.shape
    full = pieces[0].shape[1]
    wide = full // nz
    out = [jax.ShapeDtypeStruct((depth, full), BF16), jax.ShapeDtypeStruct((rows, wide), F32)]
    out += [jax.ShapeDtypeStruct((rows, wide), BF16)] * (nz - 1)
    weight, *parts = no_grid(
        functools.partial(project_value_kernel, nz),
        "s" + "v" * (1 + 2 * len(pieces)),
        out,
        [pltpu.VMEM((depth, full), BF16), pltpu.SemaphoreType.DMA],
        4 * rows * depth * full,
        2 * rows * depth + 4 * depth * full + 4 * rows * full,
        "project_value",
        pltpu.HBM,
    )(where, features, *pieces, *others)
    return weight, parts


def inverse_of(pre):
    return lax.rsqrt(jnp.mean(pre * pre, axis=-1, keepdims=True) + EPSILON)


def pack_kernel(nz, source_ref, gain_ref, *refs):
    keys, values = refs[:nz], refs[nz : 2 * nz]
    pre_ref, *outs = refs[2 * nz : -1]
    tiles = refs[-1]
    groups = len(outs)
    per_source, patch = tiles.shape[1] - 1, tiles.shape[2]
    hd = gain_ref.shape[1]
    pre_ref[...] = sum([a[...] for a in keys[1:]], keys[0][...])
    value = sum([a[...].astype(F32) for a in values[1:]], values[0][...])
    for j in range(groups):
        cols = slice(j * hd, (j + 1) * hd)
        pre = pre_ref[:, cols]
        key = (pre * inverse_of(pre) * gain_ref[...]).astype(BF16).astype(F32)
        tiles[j, :per_source, :, :hd] = key.reshape(per_source, patch, hd)
        low = value[:, cols].astype(BF16).astype(F32)
        tiles[j, :per_source, :, hd:] = low.reshape(per_source, patch, hd)
        tiles[j, per_source] = jnp.zeros(tiles.shape[2:], F32)
    capacity = outs[0].shape[1] // patch

    def fill(s, carry):
        for j in range(groups):
            rows = [tiles[j, source_ref[s * capacity + c]] for c in range(capacity)]
            outs[j][s] = jnp.concatenate(rows, axis=0).astype(BF16)
        return carry

    lax.fori_loop(0, outs[0].shape[0], fill, 0)


def pack(slot_source, gain, keys, values, n_dp, capacity, per_source, hd):
    rows, width = keys[0].shape
    patch = rows // per_source
    groups = width // hd
    out = [jax.ShapeDtypeStruct((rows, width), F32)]
    out += [jax.ShapeDtypeStruct((n_dp, capacity * patch, 2 * hd), BF16)] * groups
    pre, *sent = no_grid(
        functools.partial(pack_kernel, len(keys)),
        "sv" + "v" * (2 * len(keys)),
        out,
        [pltpu.VMEM((groups, per_source + 1, patch, 2 * hd), F32)],
        100 * rows * width,
        40 * rows * width,
        "pack",
    )(slot_source, gain, *keys, *values)
    return pre, sent


def unpack_kernel(j, slot_ref, gain_ref, home_ref, pre_ref, out_ref, terms_ref, tiles):
    per_source, patch = tiles.shape[:2]
    hd = gain_ref.shape[1]

    def fill(t, carry):
        slot = slot_ref[t]
        pair = home_ref[lax.shift_right_logical(slot, 1)].astype(F32)
        tiles[t] = jnp.where((slot & 1) == 1, pair[patch:], pair[:patch])
        return carry

    lax.fori_loop(0, per_source, fill, 0)
    both = tiles[...].reshape(per_source * patch, 2 * hd)
    grad = both[:, :hd]
    pre = pre_ref[:, j * hd : (j + 1) * hd]
    inv = inverse_of(pre)
    terms_ref[...] = jnp.sum(grad * pre * inv, axis=0, keepdims=True)
    scaled = gain_ref[...] * grad
    shared = jnp.mean(scaled * pre, axis=-1, keepdims=True)
    out_ref[:, :hd] = (inv * (scaled - pre * inv * inv * shared)).astype(BF16)
    out_ref[:, hd:] = both[:, hd:].astype(BF16)


def unpack(j, send_slot, gain, home, pre):
    rows = pre.shape[0]
    per_source = send_slot.shape[0]
    hd = gain.shape[1]
    return no_grid(
        functools.partial(unpack_kernel, j),
        "svvv",
        [jax.ShapeDtypeStruct((rows, 2 * hd), BF16), jax.ShapeDtypeStruct((1, hd), F32)],
        [pltpu.VMEM((per_source, rows // per_source, 2 * hd), F32)],
        100 * rows * hd,
        40 * rows * hd,
        "unpack",
    )(send_slot, gain, home, pre)


def weight_grad_kernel(axis, blocks, where_ref, mine_ref, theirs_ref, *refs):
    grads, others = refs[:blocks], refs[blocks : 2 * blocks]
    outs, stage = refs[2 * blocks : -1], refs[-1]
    wide = grads[0].shape[1]
    hd = wide // 2
    for i in range(blocks):
        total = dot(mine_ref[...], grads[i][...]) + dot(theirs_ref[...], others[i][...])
        stage[:, :, :, i * wide : (i + 1) * wide] = total.reshape(
            stage.shape[:3] + (wide,)
        ).astype(BF16)
    for i in range(blocks):
        owner = lax.rem(where_ref[2] + blocks - i, blocks)
        for part in range(2):
            start = pl.multiple_of((part * blocks + owner) * hd, hd)
            at = slice(i * wide + part * hd, i * wide + (part + 1) * hd)
            for d in range(len(outs)):
                to = lax.rem(where_ref[axis] + d, len(outs))
                block = stage[to, :, :, at] if axis == 0 else stage[:, to, :, at]
                outs[d][:, :, pl.ds(start, hd)] = block


def weight_grad(axis, where, mine, theirs, grads, others, nx, ny):
    cols, rows = mine.shape
    share = cols // (nx * ny)
    wide = grads[0].shape[1]
    blocks = len(grads)
    full = blocks * wide
    count, rest = (nx, ny) if axis == 0 else (ny, nx)
    return no_grid(
        functools.partial(weight_grad_kernel, axis, blocks),
        "svv" + "v" * (2 * blocks),
        [jax.ShapeDtypeStruct((rest, share, full), BF16)] * count,
        [pltpu.VMEM((nx, ny, share, full), BF16)],
        10 * rows * cols * full,
        4 * rows * cols + 4 * rows * full + 2 * cols * full,
        "weight_grad",
    )(where, mine, theirs, *grads, *others)


def feature_grad_kernel(count, *refs):
    grads, key_w, value_w, out_ref, key_g, value_g = refs[:count], *refs[count:]
    hd = grads[0].shape[1] // 2

    @pl.when(pl.program_id(0) == 0)
    def _():
        for i in range(count):
            key_g[:, i * hd : (i + 1) * hd] = grads[i][:, :hd]
            value_g[:, i * hd : (i + 1) * hd] = grads[i][:, hd:]

    total = dot_nt(key_g[...], key_w[...]) + dot_nt(value_g[...], value_w[...])
    out_ref[...] = total.astype(BF16)


def feature_grad(grads, key_w, value_w, tile):
    rows = grads[0].shape[0]
    depth, full = key_w.shape
    whole = pl.BlockSpec(grads[0].shape, lambda i: (0, 0))
    weight_spec = pl.BlockSpec((tile, full), lambda i: (i, 0))
    return pl.pallas_call(
        functools.partial(feature_grad_kernel, len(grads)),
        grid=(depth // tile,),
        in_specs=[whole] * len(grads) + [weight_spec] * 2,
        out_specs=pl.BlockSpec((rows, tile), lambda i: (0, i)),
        out_shape=jax.ShapeDtypeStruct((rows, depth), BF16),
        scratch_shapes=[pltpu.VMEM((rows, full), BF16)] * 2,
        compiler_params=pltpu.CompilerParams(
            dimension_semantics=("arbitrary",), vmem_limit_bytes=VMEM_BYTES
        ),
        cost_estimate=pl.CostEstimate(
            flops=8 * rows * depth * full,
            bytes_accessed=4 * rows * full + 4 * depth * full + 2 * rows * depth,
            transcendentals=0,
        ),
        name="feature_grad",
    )(*grads, key_w, value_w)


def slot_ranks(readers, sources, per_source):
    by_source = readers.reshape(sources, per_source)
    same_reader = by_source[:, :, None] == by_source[:, None, :]
    positions = jnp.arange(per_source, dtype=jnp.int32)
    before = positions[None, :] < positions[:, None]
    return jnp.sum(jnp.where(same_reader & before[None], 1, 0), axis=2).astype(jnp.int32)


def body(sizes, features, key_weight, value_weight, key_gain, queries, grad_out, tile_dest):
    nx, ny, nc, nz = sizes
    n_dp = nx * ny * nc
    dp, z = lax.axis_index("dp"), lax.axis_index("mp")
    core = lax.rem(dp, nc)
    py = lax.rem(dp // nc, ny)
    px = dp // (nc * ny)
    hd = key_gain.shape[0]
    rows, depth = features.shape
    width = key_weight.shape[1]
    groups = width // hd

    def z_shift(a, d):
        return lax.ppermute(a, "mp", [(i, (i + d) % nz) for i in range(nz)])

    def moved(a, dx, dy, flip=0):
        perm = []
        for i in range(n_dp):
            x, y, c = i // (ny * nc), i // nc % ny, i % nc
            perm.append((i, (((x + dx) % nx) * ny + (y + dy) % ny) * nc + (c ^ flip)))
        return lax.ppermute(a, "dp", perm)

    def swap(a):
        return moved(a, 0, 0, 1)

    x_step = lambda a, d: moved(a, d, 0)
    y_step = lambda a, d: moved(a, 0, d)
    where = jnp.stack([px, py, z])
    core_y = jnp.stack([core, py])

    def piece(weight, d, start, count):
        return lax.dynamic_slice_in_dim(weight, lax.rem(z + d, nz) * depth + start, count)

    half = depth // nc
    share = depth // n_dp
    part = half // ny
    at = core * half + py * part
    value_got = [z_shift(piece(value_weight, d, at, part), d) for d in range(1, nz)]
    value_y = jnp.concatenate([piece(value_weight, 0, at, part)] + value_got, axis=1)
    key_sent = [piece(key_weight, d, core * half, half) for d in range(1, nz)]
    key_got = [z_shift(a, d) for d, a in enumerate(key_sent, 1)]
    value_y = [value_y] + [y_step(value_y, d) for d in range(1, ny)]

    key_got, value_y = lax.optimization_barrier((key_got, value_y))
    key_other = [swap(a) for a in key_got]
    value_other = [swap(a) for a in value_y]
    key_rows_w, key_parts = project_key(
        core_y, features, piece(key_weight, 0, 0, depth), key_got, key_other
    )
    value_y[0] = after(value_y[0], key_parts[0])
    value_rows_w, value_parts = project_value(core_y, features, value_y, value_other, nz)

    by_core = features.T.reshape(nx * ny, nc, share, rows)
    mine = lax.dynamic_index_in_dim(by_core, core, 1, keepdims=False).reshape(-1, rows)
    given = lax.dynamic_index_in_dim(by_core, 1 - core, 1, keepdims=False).reshape(-1, rows)
    theirs = swap(given)

    readers = tile_dest[:, 0]
    per_source = readers.shape[0] // n_dp
    patch = rows // per_source
    capacity = max(2, (2 * per_source + n_dp - 1) // n_dp)
    ranks = slot_ranks(readers, n_dp, per_source)
    my_readers = lax.dynamic_slice_in_dim(readers, dp * per_source, per_source)
    my_ranks = lax.dynamic_index_in_dim(ranks, dp, 0, keepdims=False)
    send_slot = my_readers * capacity + my_ranks
    slots = n_dp * capacity
    fills = send_slot[None, :] == jnp.arange(slots, dtype=jnp.int32)[:, None]
    slot_source = jnp.min(
        jnp.where(fills, jnp.arange(per_source, dtype=jnp.int32)[None, :], per_source), axis=1
    )
    counts = jnp.sum(jnp.where(readers.reshape(n_dp, per_source) == dp, 1, 0), axis=1)
    live_slots = jnp.arange(capacity, dtype=jnp.int32)[None, :] < counts[:, None]
    live = jnp.broadcast_to(live_slots[:, :, None], (n_dp, capacity, patch)).reshape(-1)
    bias = jnp.where(
        live[:, None] | (jnp.arange(hd) > 0)[None, :], jnp.float32(0), jnp.float32(-1e30)
    ).astype(BF16)

    key_z = [z_shift(a, nz - d) for d, a in enumerate(key_parts[1:], 1)]
    value_z = [z_shift(a, nz - d) for d, a in enumerate(value_parts[1:], 1)]
    *key_z, value_own = lax.optimization_barrier((*key_z, value_parts[0]))
    gain = key_gain[None]
    key_pre, sent = pack(
        slot_source,
        gain,
        [key_parts[0]] + key_z,
        [value_own] + value_z,
        n_dp,
        capacity,
        per_source,
        hd,
    )

    outputs = None
    returned = []
    for j in range(groups):
        arrived = lax.all_to_all(sent[j], "dp", split_axis=0, concat_axis=0, tiled=True)
        *outputs, back = attend(
            queries, grad_out, arrived.reshape(-1, 2 * hd), bias, j, groups, hd, outputs
        )
        returned.append(back.reshape(n_dp, capacity * patch, 2 * hd))

    all_grads, first, gain_terms = [], [], []
    home = got = None
    for j in range(groups):
        back = returned[j] if home is None else after(returned[j], home)
        home = lax.all_to_all(back, "dp", split_axis=0, concat_axis=0, tiled=True)
        if got is not None:
            home = after(home, *got)
        mine_grads, terms = unpack(j, send_slot, gain, home, key_pre)
        gain_terms.append(terms)
        got = [z_shift(mine_grads, d) for d in range(1, nz)]
        grads = [mine_grads] + got
        all_grads.append(grads)
        others = [swap(g) for g in grads]
        first.append(list(weight_grad(j % 2, where, mine, theirs, grads, others, nx, ny)))

    total = jnp.broadcast_to(sum(gain_terms[1:], gain_terms[0]), (8, hd))
    for flip in (lambda i: i ^ 1, lambda i: nz - 1 - i):
        total = total + lax.ppermute(total, "mp", [(i, flip(i)) for i in range(nz)])
    total = total + swap(total)
    pair = total + y_step(total, ny // 2)
    total = pair + y_step(pair, 1)
    *first[-1], total = lax.optimization_barrier((*first[-1], total))

    def exchange(parts, step, *before):
        got = [step(parts[d], d) for d in range(1, len(parts))]
        if before:
            got, _ = lax.optimization_barrier((got, before))
        return sum([a.astype(F32) for a in got], parts[0].astype(F32))

    def split(part, place, count):
        return [
            lax.dynamic_index_in_dim(part, lax.rem(place + d, count), 0, keepdims=False)
            for d in range(count)
        ]

    sums = []
    for j in range(groups):
        if j % 2 == 0:
            mid = exchange(first[j], x_step, first[-1][0]).astype(BF16)
            total = after(total, mid)
            sums.append(exchange(split(mid, py, ny), y_step))
        else:
            mid = exchange(first[j], y_step).astype(BF16)
            sums.append(exchange(split(mid, px, nx), x_step))

    def in_order(part):
        heads = [a.reshape(share, 2, nz, hd)[:, part] for a in sums]
        return jnp.stack(heads, axis=2).reshape(share, nz * width)

    grad_key_weight, grad_value_weight = in_order(0), in_order(1)

    pair = total + x_step(total, nx // 2)
    grad_key_gain = (pair + x_step(pair, 1))[0]

    grads = [g[d] for d in range(nz) for g in all_grads]
    grad_features = feature_grad(grads, key_rows_w, value_rows_w, 256)

    return (
        outputs[0],
        outputs[1],
        grad_features,
        grad_key_weight,
        grad_value_weight,
        grad_key_gain,
    )


def solution(mesh):
    n_dp, nz = mesh.shape["dp"], mesh.shape["mp"]
    nc = 2
    ny = 4
    sizes = (n_dp // (nc * ny), ny, nc, nz)
    in_specs = (P("dp", "mp"), P(None, "mp"), P(None, "mp"), P(), P("dp", "mp"), P("dp", "mp"), P())
    out_specs = (
        P("dp", "mp"),
        P("dp", "mp"),
        P("dp", "mp"),
        P(("mp", "dp"), None),
        P(("mp", "dp"), None),
        P(),
    )
    return jax.shard_map(
        functools.partial(body, sizes),
        mesh=mesh,
        in_specs=in_specs,
        out_specs=out_specs,
        check_vma=False,
    )
```

```python
import functools
import jax
import jax.numpy as jnp
from jax import lax
from jax.experimental import pallas as pl
from jax.experimental.pallas import tpu as pltpu
from jax.sharding import PartitionSpec as P

EPSILON = 1e-05
BF16 = jnp.bfloat16
F32 = jnp.float32
LOG2E = 1.4426950408889634
VMEM_BYTES = 28 * 2**20
COST_CUT = 1000
WIDE_VMEM_BYTES = 57 * 2**20
LATE = ()
NT_DIMS = (((1,), (1,)), ((), ()))


def after(a, *others):
    return lax.optimization_barrier((a, *others))[0]


def dot(left, right):
    return jnp.dot(left, right, preferred_element_type=F32)


def dot_nt(left, right):
    return lax.dot_general(left, right, NT_DIMS, preferred_element_type=F32)


STEP_HEADS = 4


def attend_kernel(scale, steps, first, q_hbm, g_hbm, kv_ref, bias_ref, *refs):
    o_ref, gq_ref, gkv_ref, kaug, kt, vt, gk_sum, gv_sum, q_all, g_all, sems = refs[-11:]
    step = pl.program_id(0)
    hd = kt.shape[0]
    size = q_all.shape[2]
    count = size // hd

    def load(n, at):
        cols = pl.ds((first + n) * size, size)
        return [
            pltpu.make_async_copy(q_hbm.at[:, cols], q_all.at[at], sems.at[0, at]),
            pltpu.make_async_copy(g_hbm.at[:, cols], g_all.at[at], sems.at[1, at]),
        ]

    @pl.when(step == 0)
    def _():
        for n in range(steps):
            for copy in load(n, n):
                copy.start()
        kaug[:, :hd] = kv_ref[:, :hd]
        kaug[:, hd:] = bias_ref[...]
        kt[...] = kv_ref[:, :hd].T
        vt[...] = kv_ref[:, hd:].T
        gk_sum[...] = jnp.zeros_like(gk_sum)
        gv_sum[...] = jnp.zeros_like(gv_sum)

    for copy in load(0, step):
        copy.wait()
    cols = [slice(i * hd, (i + 1) * hd) for i in range(count)]
    qs = [q_all[step, :, c] for c in cols]
    gs = [g_all[step, :, c] for c in cols]
    lanes = lax.broadcasted_iota(jnp.int32, qs[0].shape, 1)
    ones = jnp.where(lanes == 0, 1.0, 0.0).astype(BF16)
    scores = [dot_nt(kaug[...], jnp.concatenate([q, ones], axis=1)) for q in qs]
    grad_probs = [dot_nt(kv_ref[:, hd:], g) for g in gs]
    lows, grad_scores = [], []
    for i in range(count):
        top = jnp.max(scores[i], axis=0, keepdims=True)
        weights = jnp.exp2((scores[i] - top) * (scale * LOG2E))
        probs = weights * (1.0 / jnp.sum(weights, axis=0, keepdims=True))
        low = probs.astype(BF16)
        out_t = dot(vt[...], low)
        delta = jnp.sum(gs[i].astype(F32).T * out_t, axis=0, keepdims=True)
        grad_low = (probs * (grad_probs[i] - delta)).astype(BF16)
        gq_t = dot(kt[...], grad_low) * scale
        o_ref[:, cols[i]] = out_t.T.astype(BF16)
        gq_ref[:, cols[i]] = gq_t.T.astype(BF16)
        lows.append(low)
        grad_scores.append(grad_low)
    gk_sum[...] += dot(jnp.concatenate(grad_scores, axis=1), jnp.concatenate(qs, axis=0))
    gv_sum[...] += dot(jnp.concatenate(lows, axis=1), jnp.concatenate(gs, axis=0))

    @pl.when(step == steps - 1)
    def _():
        gkv_ref[:, :hd] = (gk_sum[...] * scale).astype(BF16)
        gkv_ref[:, hd:] = gv_sum[...].astype(BF16)


def attend(queries, grad_out, kv, bias, group, groups, hd, so_far):
    tokens, width = queries.shape
    heads = width // hd // groups
    steps = heads // STEP_HEADS
    keys = kv.shape[0]
    by_head = pl.BlockSpec((tokens, hd * STEP_HEADS), lambda h: (0, group * steps + h))
    whole = lambda a: pl.BlockSpec(a.shape, lambda h: (0, 0))
    extra = [] if so_far is None else list(so_far)
    out = jax.ShapeDtypeStruct((tokens, width), BF16)
    return pl.pallas_call(
        functools.partial(attend_kernel, hd**-0.5, steps, group * steps),
        grid=(steps,),
        in_specs=[pl.BlockSpec(memory_space=pltpu.HBM)] * 2
        + [pl.BlockSpec((keys, 2 * hd), lambda h: (0, group)), whole(bias)]
        + [pl.BlockSpec(memory_space=pl.ANY)] * len(extra),
        out_specs=[by_head, by_head, pl.BlockSpec((keys, 2 * hd), lambda h: (0, 0))],
        out_shape=[out, out, jax.ShapeDtypeStruct((keys, 2 * hd), BF16)],
        scratch_shapes=[
            pltpu.VMEM((keys, 2 * hd), BF16),
            pltpu.VMEM((hd, keys), BF16),
            pltpu.VMEM((hd, keys), BF16),
            pltpu.VMEM((keys, hd), F32),
            pltpu.VMEM((keys, hd), F32),
            pltpu.VMEM((steps, tokens, hd * STEP_HEADS), BF16),
            pltpu.VMEM((steps, tokens, hd * STEP_HEADS), BF16),
            pltpu.SemaphoreType.DMA((2, steps)),
        ],
        input_output_aliases={} if not extra else {4: 0, 5: 1},
        compiler_params=pltpu.CompilerParams(
            dimension_semantics=("arbitrary",), vmem_limit_bytes=WIDE_VMEM_BYTES
        ),
        cost_estimate=pl.CostEstimate(
            flops=40 * heads * tokens * keys * hd,
            bytes_accessed=8 * heads * tokens * hd + 8 * keys * hd,
            transcendentals=heads * tokens * keys,
        ),
        name="attend",
    )(queries, grad_out, kv, bias, *extra)


def no_grid(
    kernel, in_specs, out_shape, scratch, flops, moved_bytes, name, first_out=None, vmem_mib=28
):
    vmem = pl.BlockSpec(memory_space=pltpu.VMEM)
    smem = pl.BlockSpec(memory_space=pltpu.SMEM)
    out_specs = [vmem] * len(out_shape)
    if first_out is not None:
        out_specs[0] = pl.BlockSpec(memory_space=first_out)
    return pl.pallas_call(
        kernel,
        in_specs=[smem if kind == "s" else vmem for kind in in_specs],
        out_specs=out_specs,
        out_shape=out_shape,
        scratch_shapes=scratch,
        compiler_params=pltpu.CompilerParams(vmem_limit_bytes=vmem_mib * 2**20),
        cost_estimate=pl.CostEstimate(
            flops=flops // COST_CUT, bytes_accessed=moved_bytes // COST_CUT, transcendentals=0
        ),
        name=name,
    )


def project_kernel(ny, at_ref, feature_ref, own_ref, *refs):
    got, other = refs[:4], refs[4:8]
    pieces, others = refs[8:13], refs[13:18]
    kept, own_key, own_value, *outs = refs[18:-2]
    weight, sem = refs[-2:]
    rows, wide = own_key.shape
    depth = weight.shape[0]
    half, size = depth // 2, pieces[0].shape[0]
    full = weight.shape[1] // 2
    weight[:, :wide] = own_ref[...]
    for core, key, value in ((at_ref[0], got, pieces), (1 - at_ref[0], other, others)):
        before, behind, far_a, far_b = key
        mine = pl.ds(pl.multiple_of(core * half, half), half)
        weight[mine, wide : 2 * wide] = before[:half]
        weight[mine, 3 * wide : full] = behind[:half]
        for n, far in enumerate((far_a, far_b)):
            some = pl.ds(pl.multiple_of(core * half + n * half // 2, half // 2), half // 2)
            weight[some, 2 * wide : 3 * wide] = far[...]
        mine, before, behind, far_a, far_b = value
        for e, n, src in (
            (0, 0, mine), (1, 0, before), (2, 0, far_a), (2, size // 2, far_b), (3, 0, behind)
        ):
            y = lax.rem(at_ref[1] + ny - e, ny)
            start = pl.multiple_of((core * ny + y) * size + n, size // 2)
            weight[pl.ds(start, src.shape[0]), full:] = src[...]
    keep = pltpu.make_async_copy(weight, kept, sem)
    keep.start()
    for d in range(4):
        key = dot(feature_ref[...], weight[:, d * wide : (d + 1) * wide])
        value = dot(feature_ref[...], weight[:, full + d * wide : full + (d + 1) * wide])
        if d == 0:
            own_key[...] = key
            own_value[...] = value
        else:
            at = 0
            for out in ((outs[0],), (outs[2], outs[3]), (outs[1],))[d - 1]:
                some = slice(at, at + out.shape[0])
                put_terms(out, slice(None), key[some], value[some])
                at += out.shape[0]
    keep.wait()


def put_terms(ref, rows, key, value):
    wide = key.shape[1]
    high = key.astype(BF16)
    ref[rows, :wide] = high
    ref[rows, wide : 2 * wide] = (key - high.astype(F32)).astype(BF16)
    ref[rows, 2 * wide :] = value.astype(BF16)


def get_terms(ref, rows=slice(None)):
    wide = ref.shape[1] // 3
    term = lambda n: ref[rows, n * wide : (n + 1) * wide].astype(F32)
    return term(0) + term(1), term(2)


def relay_kernel(prev_ref, next_ref, a_ref, b_ref, prev_out, next_out):
    cut = a_ref.shape[0]
    top, bottom = slice(0, cut), slice(cut, None)
    for src, got, out, some, rest in (
        (prev_ref, a_ref, prev_out, top, bottom),
        (next_ref, b_ref, next_out, bottom, top),
    ):
        key, value = get_terms(src, some)
        more_key, more_value = get_terms(got)
        put_terms(out, some, key + more_key, value + more_value)
        out[rest] = src[rest]


def relay(to_prev, to_next, got_a, got_b):
    size = to_prev.size
    return no_grid(
        relay_kernel,
        "vvvv",
        [jax.ShapeDtypeStruct(a.shape, a.dtype) for a in (to_prev, to_next)],
        [],
        10 * size,
        10 * size,
        "relay",
    )(to_prev, to_next, got_a, got_b)


def project(where, features, own, got, other, pieces, others, ny):
    rows, depth = features.shape
    wide = own.shape[1]
    full = pieces[0].shape[1]
    weight, own_key, own_value, *sent = no_grid(
        functools.partial(project_kernel, ny),
        "s" + "v" * (2 + 2 * len(got) + 2 * len(pieces)),
        [jax.ShapeDtypeStruct((depth, 2 * full), BF16)]
        + [jax.ShapeDtypeStruct((rows, wide), F32)] * 2
        + [jax.ShapeDtypeStruct((rows, 3 * wide), BF16)] * 2
        + [jax.ShapeDtypeStruct((rows // 2, 3 * wide), BF16)] * 2,
        [pltpu.VMEM((depth, 2 * full), BF16), pltpu.SemaphoreType.DMA],
        4 * rows * depth * full,
        2 * rows * depth + 4 * depth * full + 4 * rows * full,
        "project",
        pltpu.HBM,
        50,
    )(where, features, own, *got, *other, *pieces, *others)
    return weight, own_key, own_value, sent


def inverse_of(pre):
    return lax.rsqrt(jnp.mean(pre * pre, axis=-1, keepdims=True) + EPSILON)


def pack_kernel(source_ref, gain_ref, own_key, own_value, *refs):
    parts = refs[:-3]
    pre_ref, out_ref, tiles = refs[-3:]
    per_source, patch = tiles.shape[0] - 1, tiles.shape[1]
    hd = gain_ref.shape[1]
    terms = [get_terms(a) for a in parts]
    pre_ref[...] = sum([a for a, _ in terms], own_key[...])
    value = sum([a for _, a in terms], own_value[...])
    for j in range(pre_ref.shape[1] // hd):
        cols = slice(j * hd, (j + 1) * hd)
        pre = pre_ref[:, cols]
        key = (pre * inverse_of(pre) * gain_ref[...]).astype(BF16).astype(F32)
        low = value[:, cols].astype(BF16).astype(F32)
        both = jnp.concatenate([key, low], axis=1)
        tiles[:per_source, :, 2 * j * hd : 2 * (j + 1) * hd] = both.reshape(
            per_source, patch, 2 * hd
        )
    tiles[per_source] = jnp.zeros(tiles.shape[1:], F32)
    capacity = out_ref.shape[1] // patch

    def fill(s, carry):
        rows = [tiles[source_ref[s * capacity + c]] for c in range(capacity)]
        out_ref[s] = jnp.concatenate(rows, axis=0).astype(BF16)
        return carry

    lax.fori_loop(0, out_ref.shape[0], fill, 0)


def pack(slot_source, gain, own_key, own_value, parts, n_dp, capacity, per_source):
    rows, width = own_key.shape
    patch = rows // per_source
    return no_grid(
        pack_kernel,
        "svvv" + "v" * len(parts),
        [
            jax.ShapeDtypeStruct((rows, width), F32),
            jax.ShapeDtypeStruct((n_dp, capacity * patch, 2 * width), BF16),
        ],
        [pltpu.VMEM((per_source + 1, patch, 2 * width), F32)],
        100 * rows * width,
        40 * rows * width,
        "pack",
        None,
        57,
    )(slot_source, gain, own_key, own_value, *parts)


EXTRA = 16
HD_LANES = 128


def split_rows(total):
    hi = total.astype(BF16).astype(F32)
    mid = (total - hi).astype(BF16).astype(F32)
    low = total - hi - mid
    empty = jnp.zeros((EXTRA - 3, total.shape[1]), F32)
    return jnp.concatenate([hi, mid, low, empty], axis=0).astype(BF16)


def joined_row(rows):
    return jnp.sum(rows.astype(F32), axis=0, keepdims=True)


def unpack_kernel(j, slot_ref, gain_ref, home_ref, pre_ref, out_ref, tiles):
    per_source, patch = tiles.shape[:2]
    rows = per_source * patch
    hd = gain_ref.shape[1]

    def fill(t, carry):
        slot = slot_ref[t]
        pair = home_ref[lax.shift_right_logical(slot, 1)].astype(F32)
        tiles[t] = jnp.where((slot & 1) == 1, pair[patch:], pair[:patch])
        return carry

    lax.fori_loop(0, per_source, fill, 0)
    both = tiles[...].reshape(rows, 2 * hd)
    grad = both[:, :hd]
    pre = pre_ref[:, j * hd : (j + 1) * hd]
    inv = inverse_of(pre)
    terms = jnp.sum(grad * pre * inv, axis=0, keepdims=True)
    scaled = gain_ref[...] * grad
    shared = jnp.mean(scaled * pre, axis=-1, keepdims=True)
    out_ref[:rows, :hd] = (inv * (scaled - pre * inv * inv * shared)).astype(BF16)
    out_ref[:rows, hd:] = both[:, hd:].astype(BF16)
    out_ref[rows:, :hd] = split_rows(terms)
    out_ref[rows:, hd:] = jnp.zeros((EXTRA, hd), BF16)


def unpack(j, send_slot, gain, home, pre):
    rows = pre.shape[0]
    per_source = send_slot.shape[0]
    hd = gain.shape[1]
    return no_grid(
        functools.partial(unpack_kernel, j),
        "svvv",
        [jax.ShapeDtypeStruct((rows + EXTRA, 2 * hd), BF16)],
        [pltpu.VMEM((per_source, rows // per_source, 2 * hd), F32)],
        100 * rows * hd,
        40 * rows * hd,
        "unpack",
    )(send_slot, gain, home, pre)[0]


def weight_grad_kernel(plan, blocks, where_ref, mine_ref, theirs_ref, *refs):
    grads, others = refs[:blocks], refs[blocks : 2 * blocks]
    outs, stage = refs[2 * blocks : -1], refs[-1]
    rows = mine_ref.shape[1]
    wide = grads[0].shape[1]
    hd = wide // 2
    for i in range(blocks):
        total = dot(mine_ref[...], grads[i][:rows]) + dot(theirs_ref[...], others[i][:rows])
        stage[:, :, :, i * wide : (i + 1) * wide] = total.reshape(
            stage.shape[:3] + (wide,)
        ).astype(BF16)
    terms = split_rows(sum(joined_row(a[rows:, :hd]) for a in grads + others))
    first = 0
    for axis, parts, together in plan:
        count = stage.shape[axis]
        if together:
            each = outs[first].shape[0] // count
            mine = [outs[first].at[d * each : (d + 1) * each] for d in range(count)]
            first += 1
        else:
            mine = outs[first : first + count]
            first += count
        size = mine[0].shape[0] - EXTRA
        for d in range(count):
            to = d if together else lax.rem(where_ref[axis] + d, count)
            for i in range(blocks):
                owner = lax.rem(where_ref[2] + blocks - i, blocks)
                for n, part in enumerate(parts):
                    start = pl.multiple_of((n * blocks + owner) * hd, hd)
                    at = slice(i * wide + part * hd, i * wide + (part + 1) * hd)
                    block = stage[to, :, :, at] if axis == 0 else stage[:, to, :, at]
                    mine[d][:size, pl.ds(start, hd)] = block.reshape(size, hd)
            mine[d][size:, :hd] = terms
            mine[d][size:, hd:] = jnp.zeros((EXTRA, mine[d].shape[1] - hd), BF16)


def weight_grad(plan, where, mine, theirs, grads, others, sizes):
    cols, rows = mine.shape
    share = cols // (sizes[0] * sizes[1])
    wide = grads[0].shape[1]
    blocks = len(grads)
    full = blocks * wide
    out = []
    for axis, parts, together in plan:
        count = sizes[axis]
        each, lanes = cols // count + EXTRA, blocks * wide // 2 * len(parts)
        shapes = [(count * each, lanes)] if together else [(each, lanes)] * count
        out += [jax.ShapeDtypeStruct(shape, BF16) for shape in shapes]
    outs = no_grid(
        functools.partial(weight_grad_kernel, plan, blocks),
        "svv" + "v" * (2 * blocks),
        out,
        [pltpu.VMEM((sizes[0], sizes[1], share, full), BF16)],
        10 * rows * cols * full,
        4 * rows * cols + 4 * rows * full + 2 * cols * full,
        "weight_grad",
    )(where, mine, theirs, *grads, *others)
    grouped, first = [], 0
    for axis, _, together in plan:
        n = 1 if together else sizes[axis]
        grouped.append(list(outs[first : first + n]))
        first += n
    return grouped


def middle_kernel(axis, count, each, where_ref, *refs):
    stage = refs[-1]
    outs = refs[-count - 1 : -1]
    hd = HD_LANES
    share = stage.shape[1]
    size = share * count
    for d in range(count):
        outs[d][share:] = jnp.zeros((EXTRA, outs[d].shape[1]), BF16)
    first = at = 0
    for n in each:
        if n == 1:
            span = size + EXTRA
            group = [refs[first].at[i * span : (i + 1) * span] for i in range(refs[first].shape[0] // span)]
        else:
            group = refs[first : first + n]
        first += n
        lanes = slice(at, at + group[0].shape[1])
        total = sum(a[:size].astype(F32) for a in group)
        stage[:, :, lanes] = total.astype(BF16).reshape(count, share, -1)
        terms = split_rows(sum(joined_row(a[size:, :hd]) for a in group))
        for d in range(count):
            outs[d][share:, at : at + hd] = terms
        at = lanes.stop
    for d in range(count):
        outs[d][:share] = stage[lax.rem(where_ref[1 - axis] + d, count)]


def middle(axis, count, where, groups, share):
    cols = sum(group[0].shape[1] for group in groups)
    size = share * count
    flat = [a for group in groups for a in group]
    return list(
        no_grid(
            functools.partial(middle_kernel, axis, count, tuple(len(group) for group in groups)),
            "s" + "v" * len(flat),
            [jax.ShapeDtypeStruct((share + EXTRA, cols), BF16)] * count,
            [pltpu.VMEM((count, share, cols), BF16)],
            20 * size * cols,
            8 * size * cols,
            "middle",
        )(where, *flat)
    )


def last(plans, groups, blocks):
    share = groups[0][0].shape[0] - EXTRA
    hd = HD_LANES
    heads = 1 + max(j for plan in plans for j, _ in plan)
    full = heads * blocks * hd

    def kernel(*refs):
        outs = refs[-3:]
        first = 0
        gain = jnp.zeros((1, hd), F32)
        seen = set()
        for plan, group in zip(plans, groups):
            mine = refs[first : first + len(group)]
            first += len(group)
            total = sum(a[:share].astype(F32) for a in mine)
            at = 0
            for j, parts in plan:
                if j not in seen:
                    seen.add(j)
                    gain = gain + sum(joined_row(a[share:, at : at + hd]) for a in mine)
                for part in parts:
                    for i in range(blocks):
                        to = slice((i * heads + j) * hd, (i * heads + j + 1) * hd)
                        outs[part][:, to] = total[:, at : at + hd]
                        at += hd
        outs[2][...] = gain

    flat = [a for group in groups for a in group]
    grad = jax.ShapeDtypeStruct((share, full), F32)
    return no_grid(
        kernel,
        "v" * len(flat),
        [grad, grad, jax.ShapeDtypeStruct((1, hd), F32)],
        [],
        20 * share * full,
        24 * share * full,
        "last",
    )(*flat)


def feature_grad_kernel(count, *refs):
    grads, weight, out_ref, both = refs[:count], *refs[count:]
    rows = both.shape[0]
    hd = grads[0].shape[1] // 2
    full = count * hd

    @pl.when(pl.program_id(0) == 0)
    def _():
        for i in range(count):
            both[:, i * hd : (i + 1) * hd] = grads[i][:rows, :hd]
            both[:, full + i * hd : full + (i + 1) * hd] = grads[i][:rows, hd:]

    out_ref[...] = dot_nt(both[...], weight[...]).astype(BF16)


def feature_grad(grads, weight, tile):
    rows = grads[0].shape[0] - EXTRA
    depth, full = weight.shape
    whole = pl.BlockSpec(grads[0].shape, lambda i: (0, 0))
    return pl.pallas_call(
        functools.partial(feature_grad_kernel, len(grads)),
        grid=(depth // tile,),
        in_specs=[whole] * len(grads) + [pl.BlockSpec((tile, full), lambda i: (i, 0))],
        out_specs=pl.BlockSpec((rows, tile), lambda i: (0, i)),
        out_shape=jax.ShapeDtypeStruct((rows, depth), BF16),
        scratch_shapes=[pltpu.VMEM((rows, full), BF16)],
        compiler_params=pltpu.CompilerParams(
            dimension_semantics=("arbitrary",), vmem_limit_bytes=WIDE_VMEM_BYTES
        ),
        cost_estimate=pl.CostEstimate(
            flops=4 * rows * depth * full // COST_CUT,
            bytes_accessed=(2 * rows * full + 2 * depth * full + 2 * rows * depth) // COST_CUT,
            transcendentals=0,
        ),
        name="feature_grad",
    )(*grads, weight)


def slot_ranks(readers, sources, per_source):
    by_source = readers.reshape(sources, per_source)
    same_reader = by_source[:, :, None] == by_source[:, None, :]
    positions = jnp.arange(per_source, dtype=jnp.int32)
    before = positions[None, :] < positions[:, None]
    return jnp.sum(jnp.where(same_reader & before[None], 1, 0), axis=2).astype(jnp.int32)


def body(sizes, features, key_weight, value_weight, key_gain, queries, grad_out, tile_dest):
    nx, ny, nc, nz = sizes
    n_dp = nx * ny * nc
    dp, z = lax.axis_index("dp"), lax.axis_index("mp")
    core = lax.rem(dp, nc)
    py = lax.rem(dp // nc, ny)
    px = dp // (nc * ny)
    hd = key_gain.shape[0]
    rows, depth = features.shape
    width = key_weight.shape[1]
    groups = width // hd

    def z_shift(a, d):
        return lax.ppermute(a, "mp", [(i, (i + d) % nz) for i in range(nz)])

    def moved(a, dx, dy, flip=0):
        perm = []
        for i in range(n_dp):
            x, y, c = i // (ny * nc), i // nc % ny, i % nc
            perm.append((i, (((x + dx) % nx) * ny + (y + dy) % ny) * nc + (c ^ flip)))
        return lax.ppermute(a, "dp", perm)

    def swap(a):
        return moved(a, 0, 0, 1)

    x_step = lambda a, d: moved(a, d, 0)
    y_step = lambda a, d: moved(a, 0, d)
    where = jnp.stack([px, py, z])
    core_y = jnp.stack([core, py])

    def piece(weight, d, start, count):
        return lax.dynamic_slice_in_dim(weight, lax.rem(z + d, nz) * depth + start, count)

    half = depth // nc
    share = depth // n_dp
    part = half // ny
    at = core * half + py * part
    value_got = [z_shift(piece(value_weight, d, at, part), d) for d in range(1, nz)]
    by_core = features.T.reshape(nx * ny, nc, share, rows)
    mine = lax.dynamic_index_in_dim(by_core, core, 1, keepdims=False).reshape(-1, rows)
    given = lax.dynamic_index_in_dim(by_core, 1 - core, 1, keepdims=False).reshape(-1, rows)

    def key_piece(d, start, count):
        return piece(key_weight, d, core * half + start, count)

    quarter = half // 2
    to_next = jnp.concatenate([key_piece(1, 0, half), key_piece(2, 0, quarter)], axis=0)
    to_prev = jnp.concatenate([key_piece(nz - 1, 0, half), key_piece(2, quarter, quarter)], axis=0)
    to_next, to_prev, value_got = lax.optimization_barrier((to_next, to_prev, value_got))
    from_prev, from_next = z_shift(to_next, 1), z_shift(to_prev, nz - 1)
    value_y = jnp.concatenate([piece(value_weight, 0, at, part)] + value_got, axis=1)
    before, behind = y_step(value_y, 1), y_step(value_y, ny - 1)
    cut = part // 2
    value_y = [value_y, before, behind, y_step(before[:cut], 1), y_step(behind[cut:], ny - 1)]
    own_key = piece(key_weight, 0, 0, depth)
    from_prev, mine, theirs, own_key = lax.optimization_barrier((from_prev, mine, given, own_key))
    theirs = swap(theirs)
    far_a, far_b = z_shift(from_prev[half:], 1), z_shift(from_next[half:], nz - 1)
    early = [swap(a) for a in value_y[:3]]
    key_got, value_y = lax.optimization_barrier(([from_prev, from_next, far_a, far_b], value_y))
    key_other = [swap(a) for a in key_got]
    value_other = early + [swap(a) for a in value_y[3:]]
    weight_rows, own_key, own_value, sent_parts = project(
        core_y, features, own_key, key_got, key_other, value_y, value_other, ny
    )

    readers = tile_dest[:, 0]
    per_source = readers.shape[0] // n_dp
    patch = rows // per_source
    capacity = max(2, (2 * per_source + n_dp - 1) // n_dp)
    ranks = slot_ranks(readers, n_dp, per_source)
    my_readers = lax.dynamic_slice_in_dim(readers, dp * per_source, per_source)
    my_ranks = lax.dynamic_index_in_dim(ranks, dp, 0, keepdims=False)
    send_slot = my_readers * capacity + my_ranks
    slots = n_dp * capacity
    fills = send_slot[None, :] == jnp.arange(slots, dtype=jnp.int32)[:, None]
    slot_source = jnp.min(
        jnp.where(fills, jnp.arange(per_source, dtype=jnp.int32)[None, :], per_source), axis=1
    )
    counts = jnp.sum(jnp.where(readers.reshape(n_dp, per_source) == dp, 1, 0), axis=1)
    live_slots = jnp.arange(capacity, dtype=jnp.int32)[None, :] < counts[:, None]
    live = jnp.broadcast_to(live_slots[:, :, None], (n_dp, capacity, patch)).reshape(-1)
    bias = jnp.where(
        live[:, None] | (jnp.arange(hd) > 0)[None, :], jnp.float32(0), jnp.float32(-1e30)
    ).astype(BF16)

    to_prev, to_next, part_a, part_b = sent_parts
    to_prev, to_next = relay(to_prev, to_next, z_shift(part_a, nz - 1), z_shift(part_b, 1))
    parts = [z_shift(to_prev, nz - 1), z_shift(to_next, 1)]
    gain = key_gain[None]
    key_pre, sent = pack(
        slot_source,
        gain,
        own_key,
        own_value,
        parts,
        n_dp,
        capacity,
        per_source,
    )
    arrived = lax.all_to_all(sent, "dp", split_axis=0, concat_axis=0, tiled=True)
    arrived = arrived.reshape(slots * patch, 2 * width)

    outputs = None
    returned = []
    for j in range(groups):
        *outputs, back = attend(queries, grad_out, arrived, bias, j, groups, hd, outputs)
        returned.append(back.reshape(n_dp, capacity * patch, 2 * hd))

    lengths = (nx, ny)
    steps = (x_step, y_step)
    plans = [[(0, (0, 1), False)], [(1, (0, 1), False)]]
    all_grads, first = [], []
    home = got = None
    for j in range(groups):
        back = returned[j] if home is None else after(returned[j], home)
        home = lax.all_to_all(back, "dp", split_axis=0, concat_axis=0, tiled=True)
        if got is not None:
            home = after(home, *got)
        mine_grads = unpack(j, send_slot, gain, home, key_pre)
        got = [z_shift(mine_grads, d) for d in range(1, nz)]
        if first:
            got, _ = lax.optimization_barrier((got, first[-1]))
        all_grads.append([mine_grads] + got)
        others = [swap(g) for g in all_grads[j]]
        first.append(
            weight_grad(plans[j % 2], where, mine, theirs, all_grads[j], others, lengths)
        )

    def exchange(parts, step):
        return [parts[0]] + [step(parts[d], d) for d in range(1, len(parts))]

    first_y = exchange(first[1][0], y_step)
    late = first[0][0]
    for d in LATE:
        late[d] = after(late[d], first[1][0][0])
    first_x = exchange(late, x_step)

    grads = [g[d] for d in range(nz) for g in all_grads]
    grads[0] = after(grads[0], first[-1][0][0])
    grad_features = feature_grad(grads, weight_rows, 256)

    first_x[1] = after(first_x[1], grad_features)
    first_y[1] = after(first_y[1], grad_features)
    mid_0 = middle(0, ny, where, [first_x], share)
    mid_1 = middle(1, nx, where, [first_y], share)
    grad_key_weight, grad_value_weight, gain_sum = last(
        [[(0, (0, 1))], [(1, (0, 1))]], [exchange(mid_0, y_step), exchange(mid_1, x_step)], nz
    )

    return (
        outputs[0],
        outputs[1],
        grad_features,
        grad_key_weight,
        grad_value_weight,
        gain_sum[0],
    )


def solution(mesh):
    n_dp, nz = mesh.shape["dp"], mesh.shape["mp"]
    nc = 2
    ny = 4
    sizes = (n_dp // (nc * ny), ny, nc, nz)
    in_specs = (P("dp", "mp"), P(None, "mp"), P(None, "mp"), P(), P("dp", "mp"), P("dp", "mp"), P())
    out_specs = (
        P("dp", "mp"),
        P("dp", "mp"),
        P("dp", "mp"),
        P(("mp", "dp"), None),
        P(("mp", "dp"), None),
        P(),
    )
    return jax.shard_map(
        functools.partial(body, sizes),
        mesh=mesh,
        in_specs=in_specs,
        out_specs=out_specs,
        check_vma=False,
    )
```

```python
import functools
import jax
import jax.numpy as jnp
from jax import lax
from jax.experimental import pallas as pl
from jax.experimental.pallas import tpu as pltpu
from jax.sharding import PartitionSpec as P

EPSILON = 1e-05
BF16 = jnp.bfloat16
F32 = jnp.float32
LOG2E = 1.4426950408889634
VMEM_BYTES = 28 * 2**20
COST_CUT = 1000
WIDE_VMEM_BYTES = 57 * 2**20
LATE = ()
NT_DIMS = (((1,), (1,)), ((), ()))


def after(a, *others):
    return lax.optimization_barrier((a, *others))[0]


def dot(left, right):
    return jnp.dot(left, right, preferred_element_type=F32)


def dot_nt(left, right):
    return lax.dot_general(left, right, NT_DIMS, preferred_element_type=F32)


STEP_HEADS = 4


def attend_kernel(scale, steps, first, q_hbm, g_hbm, kv_ref, bias_ref, *refs):
    o_ref, gq_ref, gkv_ref, kaug, kt, vt, gk_sum, gv_sum, q_all, g_all, sems = refs[-11:]
    step = pl.program_id(0)
    hd = kt.shape[0]
    size = q_all.shape[2]
    count = size // hd

    def load(n, at):
        cols = pl.ds((first + n) * size, size)
        return [
            pltpu.make_async_copy(q_hbm.at[:, cols], q_all.at[at], sems.at[0, at]),
            pltpu.make_async_copy(g_hbm.at[:, cols], g_all.at[at], sems.at[1, at]),
        ]

    @pl.when(step == 0)
    def _():
        for n in range(steps):
            for copy in load(n, n):
                copy.start()
        kaug[:, :hd] = kv_ref[:, :hd]
        kaug[:, hd:] = bias_ref[...]
        kt[...] = kv_ref[:, :hd].T
        vt[...] = kv_ref[:, hd:].T
        gk_sum[...] = jnp.zeros_like(gk_sum)
        gv_sum[...] = jnp.zeros_like(gv_sum)

    for copy in load(0, step):
        copy.wait()
    cols = [slice(i * hd, (i + 1) * hd) for i in range(count)]
    qs = [q_all[step, :, c] for c in cols]
    gs = [g_all[step, :, c] for c in cols]
    lanes = lax.broadcasted_iota(jnp.int32, qs[0].shape, 1)
    ones = jnp.where(lanes == 0, 1.0, 0.0).astype(BF16)
    scores = [dot_nt(kaug[...], jnp.concatenate([q, ones], axis=1)) for q in qs]
    grad_probs = [dot_nt(kv_ref[:, hd:], g) for g in gs]
    lows, grad_scores = [], []
    for i in range(count):
        top = jnp.max(scores[i], axis=0, keepdims=True)
        weights = jnp.exp2((scores[i] - top) * (scale * LOG2E))
        probs = weights * (1.0 / jnp.sum(weights, axis=0, keepdims=True))
        low = probs.astype(BF16)
        out_t = dot(vt[...], low)
        delta = jnp.sum(gs[i].astype(F32).T * out_t, axis=0, keepdims=True)
        grad_low = (probs * (grad_probs[i] - delta)).astype(BF16)
        gq_t = dot(kt[...], grad_low) * scale
        o_ref[:, cols[i]] = out_t.T.astype(BF16)
        gq_ref[:, cols[i]] = gq_t.T.astype(BF16)
        lows.append(low)
        grad_scores.append(grad_low)
    gk_sum[...] += dot(jnp.concatenate(grad_scores, axis=1), jnp.concatenate(qs, axis=0))
    gv_sum[...] += dot(jnp.concatenate(lows, axis=1), jnp.concatenate(gs, axis=0))

    @pl.when(step == steps - 1)
    def _():
        gkv_ref[:, :hd] = (gk_sum[...] * scale).astype(BF16)
        gkv_ref[:, hd:] = gv_sum[...].astype(BF16)


def attend(queries, grad_out, kv, bias, group, groups, hd, so_far):
    tokens, width = queries.shape
    heads = width // hd // groups
    steps = heads // STEP_HEADS
    keys = kv.shape[0]
    by_head = pl.BlockSpec((tokens, hd * STEP_HEADS), lambda h: (0, group * steps + h))
    whole = lambda a: pl.BlockSpec(a.shape, lambda h: (0, 0))
    extra = [] if so_far is None else list(so_far)
    out = jax.ShapeDtypeStruct((tokens, width), BF16)
    return pl.pallas_call(
        functools.partial(attend_kernel, hd**-0.5, steps, group * steps),
        grid=(steps,),
        in_specs=[pl.BlockSpec(memory_space=pltpu.HBM)] * 2
        + [pl.BlockSpec((keys, 2 * hd), lambda h: (0, group)), whole(bias)]
        + [pl.BlockSpec(memory_space=pl.ANY)] * len(extra),
        out_specs=[by_head, by_head, pl.BlockSpec((keys, 2 * hd), lambda h: (0, 0))],
        out_shape=[out, out, jax.ShapeDtypeStruct((keys, 2 * hd), BF16)],
        scratch_shapes=[
            pltpu.VMEM((keys, 2 * hd), BF16),
            pltpu.VMEM((hd, keys), BF16),
            pltpu.VMEM((hd, keys), BF16),
            pltpu.VMEM((keys, hd), F32),
            pltpu.VMEM((keys, hd), F32),
            pltpu.VMEM((steps, tokens, hd * STEP_HEADS), BF16),
            pltpu.VMEM((steps, tokens, hd * STEP_HEADS), BF16),
            pltpu.SemaphoreType.DMA((2, steps)),
        ],
        input_output_aliases={} if not extra else {4: 0, 5: 1},
        compiler_params=pltpu.CompilerParams(
            dimension_semantics=("arbitrary",), vmem_limit_bytes=WIDE_VMEM_BYTES
        ),
        cost_estimate=pl.CostEstimate(
            flops=40 * heads * tokens * keys * hd,
            bytes_accessed=8 * heads * tokens * hd + 8 * keys * hd,
            transcendentals=heads * tokens * keys,
        ),
        name="attend",
    )(queries, grad_out, kv, bias, *extra)


def no_grid(
    kernel, in_specs, out_shape, scratch, flops, moved_bytes, name, first_out=None, vmem_mib=28
):
    vmem = pl.BlockSpec(memory_space=pltpu.VMEM)
    smem = pl.BlockSpec(memory_space=pltpu.SMEM)
    out_specs = [vmem] * len(out_shape)
    if first_out is not None:
        out_specs[0] = pl.BlockSpec(memory_space=first_out)
    return pl.pallas_call(
        kernel,
        in_specs=[smem if kind == "s" else vmem for kind in in_specs],
        out_specs=out_specs,
        out_shape=out_shape,
        scratch_shapes=scratch,
        compiler_params=pltpu.CompilerParams(vmem_limit_bytes=vmem_mib * 2**20),
        cost_estimate=pl.CostEstimate(
            flops=flops // COST_CUT, bytes_accessed=moved_bytes // COST_CUT, transcendentals=0
        ),
        name=name,
    )


def project_kernel(ny, at_ref, feature_ref, own_ref, *refs):
    got, other = refs[:4], refs[4:8]
    pieces, others = refs[8:13], refs[13:18]
    kept, own_key, own_value, *outs = refs[18:-2]
    weight, sem = refs[-2:]
    rows, wide = own_key.shape
    depth = weight.shape[0]
    half, size = depth // 2, pieces[0].shape[0]
    full = weight.shape[1] // 2
    weight[:, :wide] = own_ref[...]
    for core, key, value in ((at_ref[0], got, pieces), (1 - at_ref[0], other, others)):
        before, behind, far_a, far_b = key
        mine = pl.ds(pl.multiple_of(core * half, half), half)
        weight[mine, wide : 2 * wide] = before[:half]
        weight[mine, 3 * wide : full] = behind[:half]
        for rows, src in key_far_rows(core, half, far_a, far_b):
            weight[rows, 2 * wide : 3 * wide] = src[...]
        for rows, src in value_rows(core, at_ref[1], ny, size, value):
            weight[rows, full:] = src[...]
    keep = pltpu.make_async_copy(weight, kept, sem)
    keep.start()
    for d in (1, 3, 0):
        key = dot(feature_ref[...], weight[:, d * wide : (d + 1) * wide])
        value = dot(feature_ref[...], weight[:, full + d * wide : full + (d + 1) * wide])
        if d == 0:
            own_key[...] = key
            own_value[...] = value
        else:
            put_terms(outs[d // 2], slice(None), key, value)
    keep.wait()


def key_far_rows(core, half, far_a, far_b):
    size = half // 2
    for n, src in enumerate((far_a, far_b)):
        yield pl.ds(pl.multiple_of(core * half + n * size, size), size), src


def value_rows(core, at, ny, size, pieces):
    mine, before, behind, far_a, far_b = pieces
    for e, n, src in (
        (0, 0, mine), (1, 0, before), (2, 0, far_a), (2, size // 2, far_b), (3, 0, behind)
    ):
        y = lax.rem(at + ny - e, ny)
        start = pl.multiple_of((core * ny + y) * size + n, size // 2)
        yield pl.ds(start, src.shape[0]), src


def project_far_kernel(ny, at_ref, feature_ref, *refs):
    got, other = refs[:2], refs[2:4]
    pieces, others = refs[4:9], refs[9:14]
    outs, weight = refs[14:16], refs[16]
    wide = got[0].shape[1]
    half, size = weight.shape[0] // 2, pieces[0].shape[0]
    for core, key, value in ((at_ref[0], got, pieces), (1 - at_ref[0], other, others)):
        for rows, src in key_far_rows(core, half, *key):
            weight[rows, :wide] = src[...]
        for rows, src in value_rows(core, at_ref[1], ny, size, value):
            weight[rows, wide:] = src[:, 2 * wide : 3 * wide]
    both = dot(feature_ref[...], weight[...])
    cut = outs[0].shape[0]
    for n, out in enumerate(outs):
        some = slice(n * cut, (n + 1) * cut)
        put_terms(out, slice(None), both[some, :wide], both[some, wide:])


def project_far(where, features, got, other, pieces, others, ny):
    rows, depth = features.shape
    wide = got[0].shape[1]
    return no_grid(
        functools.partial(project_far_kernel, ny),
        "s" + "v" * (1 + 2 * len(got) + 2 * len(pieces)),
        [jax.ShapeDtypeStruct((rows // 2, 3 * wide), BF16)] * 2,
        [pltpu.VMEM((depth, 2 * wide), BF16)],
        4 * rows * depth * wide,
        2 * rows * depth + 4 * depth * wide + 6 * rows * wide,
        "project_far",
        None,
        57,
    )(where, features, *got, *other, *pieces, *others)


def put_terms(ref, rows, key, value):
    wide = key.shape[1]
    high = key.astype(BF16)
    ref[rows, :wide] = high
    ref[rows, wide : 2 * wide] = (key - high.astype(F32)).astype(BF16)
    ref[rows, 2 * wide :] = value.astype(BF16)


def get_terms(ref, rows=slice(None)):
    wide = ref.shape[1] // 3
    term = lambda n: ref[rows, n * wide : (n + 1) * wide].astype(F32)
    return term(0) + term(1), term(2)


def relay_kernel(prev_ref, next_ref, a_ref, b_ref, prev_out, next_out):
    cut = a_ref.shape[0]
    top, bottom = slice(0, cut), slice(cut, None)
    for src, got, out, some, rest in (
        (prev_ref, a_ref, prev_out, top, bottom),
        (next_ref, b_ref, next_out, bottom, top),
    ):
        key, value = get_terms(src, some)
        more_key, more_value = get_terms(got)
        put_terms(out, some, key + more_key, value + more_value)
        out[rest] = src[rest]


def relay(to_prev, to_next, got_a, got_b):
    size = to_prev.size
    return no_grid(
        relay_kernel,
        "vvvv",
        [jax.ShapeDtypeStruct(a.shape, a.dtype) for a in (to_prev, to_next)],
        [],
        10 * size,
        10 * size,
        "relay",
        None,
        57,
    )(to_prev, to_next, got_a, got_b)


def project(where, features, own, got, other, pieces, others, ny):
    rows, depth = features.shape
    wide = own.shape[1]
    full = pieces[0].shape[1]
    weight, own_key, own_value, *sent = no_grid(
        functools.partial(project_kernel, ny),
        "s" + "v" * (2 + 2 * len(got) + 2 * len(pieces)),
        [jax.ShapeDtypeStruct((depth, 2 * full), BF16)]
        + [jax.ShapeDtypeStruct((rows, wide), F32)] * 2
        + [jax.ShapeDtypeStruct((rows, 3 * wide), BF16)] * 2,
        [pltpu.VMEM((depth, 2 * full), BF16), pltpu.SemaphoreType.DMA],
        4 * rows * depth * full,
        2 * rows * depth + 4 * depth * full + 4 * rows * full,
        "project",
        pltpu.HBM,
        57,
    )(where, features, own, *got, *other, *pieces, *others)
    return weight, own_key, own_value, sent


def inverse_of(pre):
    return lax.rsqrt(jnp.mean(pre * pre, axis=-1, keepdims=True) + EPSILON)


def pack_kernel(source_ref, gain_ref, own_key, own_value, *refs):
    parts = refs[:-3]
    pre_ref, out_ref, tiles = refs[-3:]
    per_source, patch = tiles.shape[0] - 1, tiles.shape[1]
    hd = gain_ref.shape[1]
    terms = [get_terms(a) for a in parts]
    pre_ref[...] = sum([a for a, _ in terms], own_key[...])
    value = sum([a for _, a in terms], own_value[...])
    for j in range(pre_ref.shape[1] // hd):
        cols = slice(j * hd, (j + 1) * hd)
        pre = pre_ref[:, cols]
        key = (pre * inverse_of(pre) * gain_ref[...]).astype(BF16).astype(F32)
        low = value[:, cols].astype(BF16).astype(F32)
        both = jnp.concatenate([key, low], axis=1)
        tiles[:per_source, :, 2 * j * hd : 2 * (j + 1) * hd] = both.reshape(
            per_source, patch, 2 * hd
        )
    tiles[per_source] = jnp.zeros(tiles.shape[1:], F32)
    capacity = out_ref.shape[1] // patch

    def fill(s, carry):
        rows = [tiles[source_ref[s * capacity + c]] for c in range(capacity)]
        out_ref[s] = jnp.concatenate(rows, axis=0).astype(BF16)
        return carry

    lax.fori_loop(0, out_ref.shape[0], fill, 0)


def pack(slot_source, gain, own_key, own_value, parts, n_dp, capacity, per_source):
    rows, width = own_key.shape
    patch = rows // per_source
    return no_grid(
        pack_kernel,
        "svvv" + "v" * len(parts),
        [
            jax.ShapeDtypeStruct((rows, width), F32),
            jax.ShapeDtypeStruct((n_dp, capacity * patch, 2 * width), BF16),
        ],
        [pltpu.VMEM((per_source + 1, patch, 2 * width), F32)],
        100 * rows * width,
        40 * rows * width,
        "pack",
        None,
        57,
    )(slot_source, gain, own_key, own_value, *parts)


EXTRA = 16
HD_LANES = 128


def split_rows(total):
    hi = total.astype(BF16).astype(F32)
    mid = (total - hi).astype(BF16).astype(F32)
    low = total - hi - mid
    empty = jnp.zeros((EXTRA - 3, total.shape[1]), F32)
    return jnp.concatenate([hi, mid, low, empty], axis=0).astype(BF16)


def joined_row(rows):
    return jnp.sum(rows.astype(F32), axis=0, keepdims=True)


def unpack_kernel(j, slot_ref, gain_ref, home_ref, pre_ref, out_ref, tiles):
    per_source, patch = tiles.shape[:2]
    rows = per_source * patch
    hd = gain_ref.shape[1]

    def fill(t, carry):
        slot = slot_ref[t]
        pair = home_ref[lax.shift_right_logical(slot, 1)].astype(F32)
        tiles[t] = jnp.where((slot & 1) == 1, pair[patch:], pair[:patch])
        return carry

    lax.fori_loop(0, per_source, fill, 0)
    both = tiles[...].reshape(rows, 2 * hd)
    grad = both[:, :hd]
    pre = pre_ref[:, j * hd : (j + 1) * hd]
    inv = inverse_of(pre)
    terms = jnp.sum(grad * pre * inv, axis=0, keepdims=True)
    scaled = gain_ref[...] * grad
    shared = jnp.mean(scaled * pre, axis=-1, keepdims=True)
    out_ref[:rows, :hd] = (inv * (scaled - pre * inv * inv * shared)).astype(BF16)
    out_ref[:rows, hd:] = both[:, hd:].astype(BF16)
    out_ref[rows:, :hd] = split_rows(terms)
    out_ref[rows:, hd:] = jnp.zeros((EXTRA, hd), BF16)


def unpack(j, send_slot, gain, home, pre):
    rows = pre.shape[0]
    per_source = send_slot.shape[0]
    hd = gain.shape[1]
    return no_grid(
        functools.partial(unpack_kernel, j),
        "svvv",
        [jax.ShapeDtypeStruct((rows + EXTRA, 2 * hd), BF16)],
        [pltpu.VMEM((per_source, rows // per_source, 2 * hd), F32)],
        100 * rows * hd,
        40 * rows * hd,
        "unpack",
    )(send_slot, gain, home, pre)[0]


def weight_grad_kernel(plan, blocks, where_ref, mine_ref, theirs_ref, *refs):
    grads, others = refs[:blocks], refs[blocks : 2 * blocks]
    outs, stage = refs[2 * blocks : -1], refs[-1]
    rows = mine_ref.shape[1]
    wide = grads[0].shape[1]
    hd = wide // 2
    for i in range(blocks):
        total = dot(mine_ref[...], grads[i][:rows]) + dot(theirs_ref[...], others[i][:rows])
        stage[:, :, :, i * wide : (i + 1) * wide] = total.reshape(
            stage.shape[:3] + (wide,)
        ).astype(BF16)
    terms = split_rows(sum(joined_row(a[rows:, :hd]) for a in grads + others))
    first = 0
    for axis, parts, together in plan:
        count = stage.shape[axis]
        if together:
            each = outs[first].shape[0] // count
            mine = [outs[first].at[d * each : (d + 1) * each] for d in range(count)]
            first += 1
        else:
            mine = outs[first : first + count]
            first += count
        size = mine[0].shape[0] - EXTRA
        for d in range(count):
            to = d if together else lax.rem(where_ref[axis] + d, count)
            for i in range(blocks):
                owner = lax.rem(where_ref[2] + blocks - i, blocks)
                for n, part in enumerate(parts):
                    start = pl.multiple_of((n * blocks + owner) * hd, hd)
                    at = slice(i * wide + part * hd, i * wide + (part + 1) * hd)
                    block = stage[to, :, :, at] if axis == 0 else stage[:, to, :, at]
                    mine[d][:size, pl.ds(start, hd)] = block.reshape(size, hd)
            mine[d][size:, :hd] = terms
            mine[d][size:, hd:] = jnp.zeros((EXTRA, mine[d].shape[1] - hd), BF16)


def weight_grad(plan, where, mine, theirs, grads, others, sizes):
    cols, rows = mine.shape
    share = cols // (sizes[0] * sizes[1])
    wide = grads[0].shape[1]
    blocks = len(grads)
    full = blocks * wide
    out = []
    for axis, parts, together in plan:
        count = sizes[axis]
        each, lanes = cols // count + EXTRA, blocks * wide // 2 * len(parts)
        shapes = [(count * each, lanes)] if together else [(each, lanes)] * count
        out += [jax.ShapeDtypeStruct(shape, BF16) for shape in shapes]
    outs = no_grid(
        functools.partial(weight_grad_kernel, plan, blocks),
        "svv" + "v" * (2 * blocks),
        out,
        [pltpu.VMEM((sizes[0], sizes[1], share, full), BF16)],
        10 * rows * cols * full,
        4 * rows * cols + 4 * rows * full + 2 * cols * full,
        "weight_grad",
    )(where, mine, theirs, *grads, *others)
    grouped, first = [], 0
    for axis, _, together in plan:
        n = 1 if together else sizes[axis]
        grouped.append(list(outs[first : first + n]))
        first += n
    return grouped


def middle_kernel(axis, count, each, where_ref, *refs):
    stage = refs[-1]
    outs = refs[-count - 1 : -1]
    hd = HD_LANES
    share = stage.shape[1]
    size = share * count
    for d in range(count):
        outs[d][share:] = jnp.zeros((EXTRA, outs[d].shape[1]), BF16)
    first = at = 0
    for n in each:
        if n == 1:
            span = size + EXTRA
            group = [refs[first].at[i * span : (i + 1) * span] for i in range(refs[first].shape[0] // span)]
        else:
            group = refs[first : first + n]
        first += n
        lanes = slice(at, at + group[0].shape[1])
        total = sum(a[:size].astype(F32) for a in group)
        stage[:, :, lanes] = total.astype(BF16).reshape(count, share, -1)
        terms = split_rows(sum(joined_row(a[size:, :hd]) for a in group))
        for d in range(count):
            outs[d][share:, at : at + hd] = terms
        at = lanes.stop
    for d in range(count):
        outs[d][:share] = stage[lax.rem(where_ref[1 - axis] + d, count)]


def middle(axis, count, where, groups, share):
    cols = sum(group[0].shape[1] for group in groups)
    size = share * count
    flat = [a for group in groups for a in group]
    return list(
        no_grid(
            functools.partial(middle_kernel, axis, count, tuple(len(group) for group in groups)),
            "s" + "v" * len(flat),
            [jax.ShapeDtypeStruct((share + EXTRA, cols), BF16)] * count,
            [pltpu.VMEM((count, share, cols), BF16)],
            20 * size * cols,
            8 * size * cols,
            "middle",
        )(where, *flat)
    )


def last(plans, groups, blocks):
    share = groups[0][0].shape[0] - EXTRA
    hd = HD_LANES
    heads = 1 + max(j for plan in plans for j, _ in plan)
    full = heads * blocks * hd

    def kernel(*refs):
        outs = refs[-3:]
        first = 0
        gain = jnp.zeros((1, hd), F32)
        seen = set()
        for plan, group in zip(plans, groups):
            mine = refs[first : first + len(group)]
            first += len(group)
            total = sum(a[:share].astype(F32) for a in mine)
            at = 0
            for j, parts in plan:
                if j not in seen:
                    seen.add(j)
                    gain = gain + sum(joined_row(a[share:, at : at + hd]) for a in mine)
                for part in parts:
                    for i in range(blocks):
                        to = slice((i * heads + j) * hd, (i * heads + j + 1) * hd)
                        outs[part][:, to] = total[:, at : at + hd]
                        at += hd
        outs[2][...] = gain

    flat = [a for group in groups for a in group]
    grad = jax.ShapeDtypeStruct((share, full), F32)
    return no_grid(
        kernel,
        "v" * len(flat),
        [grad, grad, jax.ShapeDtypeStruct((1, hd), F32)],
        [],
        20 * share * full,
        24 * share * full,
        "last",
    )(*flat)


def feature_grad_kernel(count, *refs):
    grads, weight, out_ref, both = refs[:count], *refs[count:]
    rows = both.shape[0]
    hd = grads[0].shape[1] // 2
    full = count * hd

    @pl.when(pl.program_id(0) == 0)
    def _():
        for i in range(count):
            both[:, i * hd : (i + 1) * hd] = grads[i][:rows, :hd]
            both[:, full + i * hd : full + (i + 1) * hd] = grads[i][:rows, hd:]

    out_ref[...] = dot_nt(both[...], weight[...]).astype(BF16)


def feature_grad(grads, weight, tile):
    rows = grads[0].shape[0] - EXTRA
    depth, full = weight.shape
    whole = pl.BlockSpec(grads[0].shape, lambda i: (0, 0))
    return pl.pallas_call(
        functools.partial(feature_grad_kernel, len(grads)),
        grid=(depth // tile,),
        in_specs=[whole] * len(grads) + [pl.BlockSpec((tile, full), lambda i: (i, 0))],
        out_specs=pl.BlockSpec((rows, tile), lambda i: (0, i)),
        out_shape=jax.ShapeDtypeStruct((rows, depth), BF16),
        scratch_shapes=[pltpu.VMEM((rows, full), BF16)],
        compiler_params=pltpu.CompilerParams(
            dimension_semantics=("arbitrary",), vmem_limit_bytes=WIDE_VMEM_BYTES
        ),
        cost_estimate=pl.CostEstimate(
            flops=4 * rows * depth * full // COST_CUT,
            bytes_accessed=(2 * rows * full + 2 * depth * full + 2 * rows * depth) // COST_CUT,
            transcendentals=0,
        ),
        name="feature_grad",
    )(*grads, weight)


def slot_ranks(readers, sources, per_source):
    by_source = readers.reshape(sources, per_source)
    same_reader = by_source[:, :, None] == by_source[:, None, :]
    positions = jnp.arange(per_source, dtype=jnp.int32)
    before = positions[None, :] < positions[:, None]
    return jnp.sum(jnp.where(same_reader & before[None], 1, 0), axis=2).astype(jnp.int32)


def body(sizes, features, key_weight, value_weight, key_gain, queries, grad_out, tile_dest):
    nx, ny, nc, nz = sizes
    n_dp = nx * ny * nc
    dp, z = lax.axis_index("dp"), lax.axis_index("mp")
    core = lax.rem(dp, nc)
    py = lax.rem(dp // nc, ny)
    px = dp // (nc * ny)
    hd = key_gain.shape[0]
    rows, depth = features.shape
    width = key_weight.shape[1]
    groups = width // hd

    def z_shift(a, d):
        return lax.ppermute(a, "mp", [(i, (i + d) % nz) for i in range(nz)])

    def moved(a, dx, dy, flip=0):
        perm = []
        for i in range(n_dp):
            x, y, c = i // (ny * nc), i // nc % ny, i % nc
            perm.append((i, (((x + dx) % nx) * ny + (y + dy) % ny) * nc + (c ^ flip)))
        return lax.ppermute(a, "dp", perm)

    def swap(a):
        return moved(a, 0, 0, 1)

    x_step = lambda a, d: moved(a, d, 0)
    y_step = lambda a, d: moved(a, 0, d)
    where = jnp.stack([px, py, z])
    core_y = jnp.stack([core, py])

    def piece(weight, d, start, count):
        return lax.dynamic_slice_in_dim(weight, lax.rem(z + d, nz) * depth + start, count)

    half = depth // nc
    share = depth // n_dp
    part = half // ny
    at = core * half + py * part
    value_got = [z_shift(piece(value_weight, d, at, part), d) for d in range(1, nz)]
    by_core = features.T.reshape(nx * ny, nc, share, rows)
    mine = lax.dynamic_index_in_dim(by_core, core, 1, keepdims=False).reshape(-1, rows)
    given = lax.dynamic_index_in_dim(by_core, 1 - core, 1, keepdims=False).reshape(-1, rows)

    def key_piece(d, start, count):
        return piece(key_weight, d, core * half + start, count)

    quarter = half // 2
    to_next = jnp.concatenate([key_piece(1, 0, half), key_piece(2, 0, quarter)], axis=0)
    to_prev = jnp.concatenate([key_piece(nz - 1, 0, half), key_piece(2, quarter, quarter)], axis=0)
    to_next, to_prev, value_got = lax.optimization_barrier((to_next, to_prev, value_got))
    from_prev, from_next = z_shift(to_next, 1), z_shift(to_prev, nz - 1)
    value_y = jnp.concatenate([piece(value_weight, 0, at, part)] + value_got, axis=1)
    before, behind = y_step(value_y, 1), y_step(value_y, ny - 1)
    cut = part // 2
    value_y = [value_y, before, behind, y_step(before[:cut], 1), y_step(behind[cut:], ny - 1)]
    own_key = piece(key_weight, 0, 0, depth)
    from_prev, mine, theirs, own_key = lax.optimization_barrier((from_prev, mine, given, own_key))
    theirs = swap(theirs)
    far_a, far_b = z_shift(from_prev[half:], 1), z_shift(from_next[half:], nz - 1)
    early = [swap(a) for a in value_y[:3]]
    key_got, value_y = lax.optimization_barrier(([from_prev, from_next, far_a, far_b], value_y))
    far_other = [swap(a) for a in key_got[2:]]
    value_other = early + [swap(a) for a in value_y[3:]]
    near, far_other, value_other[3:] = lax.optimization_barrier(
        (key_got[:2], far_other, value_other[3:])
    )
    key_other = [swap(a) for a in near] + far_other
    part_a, part_b = project_far(
        core_y, features, key_got[2:], key_other[2:], value_y, value_other, ny
    )
    got_a, got_b = z_shift(part_a, nz - 1), z_shift(part_b, 1)
    key_got[0] = after(key_got[0], part_a)
    weight_rows, own_key, own_value, (to_prev, to_next) = project(
        core_y, features, own_key, key_got, key_other, value_y, value_other, ny
    )
    got_a, got_b, _ = lax.optimization_barrier((got_a, got_b, to_prev))

    readers = tile_dest[:, 0]
    per_source = readers.shape[0] // n_dp
    patch = rows // per_source
    capacity = max(2, (2 * per_source + n_dp - 1) // n_dp)
    ranks = slot_ranks(readers, n_dp, per_source)
    my_readers = lax.dynamic_slice_in_dim(readers, dp * per_source, per_source)
    my_ranks = lax.dynamic_index_in_dim(ranks, dp, 0, keepdims=False)
    send_slot = my_readers * capacity + my_ranks
    slots = n_dp * capacity
    fills = send_slot[None, :] == jnp.arange(slots, dtype=jnp.int32)[:, None]
    slot_source = jnp.min(
        jnp.where(fills, jnp.arange(per_source, dtype=jnp.int32)[None, :], per_source), axis=1
    )
    counts = jnp.sum(jnp.where(readers.reshape(n_dp, per_source) == dp, 1, 0), axis=1)
    live_slots = jnp.arange(capacity, dtype=jnp.int32)[None, :] < counts[:, None]
    live = jnp.broadcast_to(live_slots[:, :, None], (n_dp, capacity, patch)).reshape(-1)
    bias = jnp.where(
        live[:, None] | (jnp.arange(hd) > 0)[None, :], jnp.float32(0), jnp.float32(-1e30)
    ).astype(BF16)

    to_prev, to_next = relay(to_prev, to_next, got_a, got_b)
    parts = [z_shift(to_prev, nz - 1), z_shift(to_next, 1)]
    gain = key_gain[None]
    key_pre, sent = pack(
        slot_source,
        gain,
        own_key,
        own_value,
        parts,
        n_dp,
        capacity,
        per_source,
    )
    arrived = lax.all_to_all(sent, "dp", split_axis=0, concat_axis=0, tiled=True)
    arrived = arrived.reshape(slots * patch, 2 * width)

    outputs = None
    returned = []
    for j in range(groups):
        *outputs, back = attend(queries, grad_out, arrived, bias, j, groups, hd, outputs)
        returned.append(back.reshape(n_dp, capacity * patch, 2 * hd))

    lengths = (nx, ny)
    steps = (x_step, y_step)
    plans = [[(0, (0, 1), False)], [(1, (0, 1), False)]]
    all_grads, first = [], []
    home = got = None
    for j in range(groups):
        back = returned[j] if home is None else after(returned[j], home)
        home = lax.all_to_all(back, "dp", split_axis=0, concat_axis=0, tiled=True)
        if got is not None:
            home = after(home, *got)
        mine_grads = unpack(j, send_slot, gain, home, key_pre)
        got = [z_shift(mine_grads, d) for d in range(1, nz)]
        if first:
            got, _ = lax.optimization_barrier((got, first[-1]))
        all_grads.append([mine_grads] + got)
        others = [swap(g) for g in all_grads[j]]
        first.append(
            weight_grad(plans[j % 2], where, mine, theirs, all_grads[j], others, lengths)
        )

    def exchange(parts, step):
        return [parts[0]] + [step(parts[d], d) for d in range(1, len(parts))]

    first_y = exchange(first[1][0], y_step)
    late = first[0][0]
    for d in LATE:
        late[d] = after(late[d], first[1][0][0])
    first_x = exchange(late, x_step)

    grads = [g[d] for d in range(nz) for g in all_grads]
    grads[0] = after(grads[0], first[-1][0][0])
    grad_features = feature_grad(grads, weight_rows, 256)

    first_x[1] = after(first_x[1], grad_features)
    first_y[1] = after(first_y[1], grad_features)
    mid_0 = middle(0, ny, where, [first_x], share)
    mid_1 = middle(1, nx, where, [first_y], share)
    grad_key_weight, grad_value_weight, gain_sum = last(
        [[(0, (0, 1))], [(1, (0, 1))]], [exchange(mid_0, y_step), exchange(mid_1, x_step)], nz
    )

    return (
        outputs[0],
        outputs[1],
        grad_features,
        grad_key_weight,
        grad_value_weight,
        gain_sum[0],
    )


def solution(mesh):
    n_dp, nz = mesh.shape["dp"], mesh.shape["mp"]
    nc = 2
    ny = 4
    sizes = (n_dp // (nc * ny), ny, nc, nz)
    in_specs = (P("dp", "mp"), P(None, "mp"), P(None, "mp"), P(), P("dp", "mp"), P("dp", "mp"), P())
    out_specs = (
        P("dp", "mp"),
        P("dp", "mp"),
        P("dp", "mp"),
        P(("mp", "dp"), None),
        P(("mp", "dp"), None),
        P(),
    )
    return jax.shard_map(
        functools.partial(body, sizes),
        mesh=mesh,
        in_specs=in_specs,
        out_specs=out_specs,
        check_vma=False,
    )
```

```python
import functools
import jax
import jax.numpy as jnp
from jax import lax
from jax.experimental import pallas as pl
from jax.experimental.pallas import tpu as pltpu
from jax.sharding import PartitionSpec as P

EPSILON = 1e-05
BF16 = jnp.bfloat16
F32 = jnp.float32
LOG2E = 1.4426950408889634
VMEM_BYTES = 28 * 2**20
COST_CUT = 1000
WIDE_VMEM_BYTES = 57 * 2**20
LATE = ()
NT_DIMS = (((1,), (1,)), ((), ()))


def after(a, *others):
    return lax.optimization_barrier((a, *others))[0]


def dot(left, right):
    return jnp.dot(left, right, preferred_element_type=F32)


def dot_nt(left, right):
    return lax.dot_general(left, right, NT_DIMS, preferred_element_type=F32)


STEP_HEADS = 4


def attend_kernel(scale, steps, first, q_hbm, g_hbm, kv_ref, bias_ref, *refs):
    o_ref, gq_ref, gkv_ref, kaug, kt, vt, gk_sum, gv_sum, q_all, g_all, sems = refs[-11:]
    step = pl.program_id(0)
    hd = kt.shape[0]
    size = q_all.shape[2]
    count = size // hd

    def load(n, at):
        cols = pl.ds((first + n) * size, size)
        return [
            pltpu.make_async_copy(q_hbm.at[:, cols], q_all.at[at], sems.at[0, at]),
            pltpu.make_async_copy(g_hbm.at[:, cols], g_all.at[at], sems.at[1, at]),
        ]

    @pl.when(step == 0)
    def _():
        for n in range(steps):
            for copy in load(n, n):
                copy.start()
        kaug[:, :hd] = kv_ref[:, :hd]
        kaug[:, hd:] = bias_ref[...]
        kt[...] = kv_ref[:, :hd].T
        vt[...] = kv_ref[:, hd:].T
        gk_sum[...] = jnp.zeros_like(gk_sum)
        gv_sum[...] = jnp.zeros_like(gv_sum)

    for copy in load(0, step):
        copy.wait()
    cols = [slice(i * hd, (i + 1) * hd) for i in range(count)]
    qs = [q_all[step, :, c] for c in cols]
    gs = [g_all[step, :, c] for c in cols]
    lanes = lax.broadcasted_iota(jnp.int32, qs[0].shape, 1)
    ones = jnp.where(lanes == 0, 1.0, 0.0).astype(BF16)
    scores = [dot_nt(kaug[...], jnp.concatenate([q, ones], axis=1)) for q in qs]
    grad_probs = [dot_nt(kv_ref[:, hd:], g) for g in gs]
    lows, grad_scores = [], []
    for i in range(count):
        top = jnp.max(scores[i], axis=0, keepdims=True)
        weights = jnp.exp2((scores[i] - top) * (scale * LOG2E))
        probs = weights * (1.0 / jnp.sum(weights, axis=0, keepdims=True))
        low = probs.astype(BF16)
        out_t = dot(vt[...], low)
        delta = jnp.sum(gs[i].astype(F32).T * out_t, axis=0, keepdims=True)
        grad_low = (probs * (grad_probs[i] - delta)).astype(BF16)
        gq_t = dot(kt[...], grad_low) * scale
        o_ref[:, cols[i]] = out_t.T.astype(BF16)
        gq_ref[:, cols[i]] = gq_t.T.astype(BF16)
        lows.append(low)
        grad_scores.append(grad_low)
    gk_sum[...] += dot(jnp.concatenate(grad_scores, axis=1), jnp.concatenate(qs, axis=0))
    gv_sum[...] += dot(jnp.concatenate(lows, axis=1), jnp.concatenate(gs, axis=0))

    @pl.when(step == steps - 1)
    def _():
        gkv_ref[:, :hd] = (gk_sum[...] * scale).astype(BF16)
        gkv_ref[:, hd:] = gv_sum[...].astype(BF16)


def attend(queries, grad_out, kv, bias, group, groups, hd, so_far):
    tokens, width = queries.shape
    heads = width // hd // groups
    steps = heads // STEP_HEADS
    keys = kv.shape[0]
    by_head = pl.BlockSpec((tokens, hd * STEP_HEADS), lambda h: (0, group * steps + h))
    whole = lambda a: pl.BlockSpec(a.shape, lambda h: (0, 0))
    extra = [] if so_far is None else list(so_far)
    out = jax.ShapeDtypeStruct((tokens, width), BF16)
    return pl.pallas_call(
        functools.partial(attend_kernel, hd**-0.5, steps, group * steps),
        grid=(steps,),
        in_specs=[pl.BlockSpec(memory_space=pltpu.HBM)] * 2
        + [pl.BlockSpec((keys, 2 * hd), lambda h: (0, group)), whole(bias)]
        + [pl.BlockSpec(memory_space=pl.ANY)] * len(extra),
        out_specs=[by_head, by_head, pl.BlockSpec((keys, 2 * hd), lambda h: (0, 0))],
        out_shape=[out, out, jax.ShapeDtypeStruct((keys, 2 * hd), BF16)],
        scratch_shapes=[
            pltpu.VMEM((keys, 2 * hd), BF16),
            pltpu.VMEM((hd, keys), BF16),
            pltpu.VMEM((hd, keys), BF16),
            pltpu.VMEM((keys, hd), F32),
            pltpu.VMEM((keys, hd), F32),
            pltpu.VMEM((steps, tokens, hd * STEP_HEADS), BF16),
            pltpu.VMEM((steps, tokens, hd * STEP_HEADS), BF16),
            pltpu.SemaphoreType.DMA((2, steps)),
        ],
        input_output_aliases={} if not extra else {4: 0, 5: 1},
        compiler_params=pltpu.CompilerParams(
            dimension_semantics=("arbitrary",), vmem_limit_bytes=WIDE_VMEM_BYTES
        ),
        cost_estimate=pl.CostEstimate(
            flops=40 * heads * tokens * keys * hd,
            bytes_accessed=8 * heads * tokens * hd + 8 * keys * hd,
            transcendentals=heads * tokens * keys,
        ),
        name="attend",
    )(queries, grad_out, kv, bias, *extra)


def no_grid(
    kernel, in_specs, out_shape, scratch, flops, moved_bytes, name, first_out=None, vmem_mib=28
):
    vmem = pl.BlockSpec(memory_space=pltpu.VMEM)
    smem = pl.BlockSpec(memory_space=pltpu.SMEM)
    out_specs = [vmem] * len(out_shape)
    if first_out is not None:
        out_specs[0] = pl.BlockSpec(memory_space=first_out)
    return pl.pallas_call(
        kernel,
        in_specs=[smem if kind == "s" else vmem for kind in in_specs],
        out_specs=out_specs,
        out_shape=out_shape,
        scratch_shapes=scratch,
        compiler_params=pltpu.CompilerParams(vmem_limit_bytes=vmem_mib * 2**20),
        cost_estimate=pl.CostEstimate(
            flops=flops // COST_CUT, bytes_accessed=moved_bytes // COST_CUT, transcendentals=0
        ),
        name=name,
    )


def project_kernel(ny, at_ref, feature_ref, own_ref, *refs):
    got, other = refs[:4], refs[4:8]
    pieces, others = refs[8:13], refs[13:18]
    kept, own_key, own_value, *outs = refs[18:-2]
    weight, sem = refs[-2:]
    rows, wide = own_key.shape
    depth = weight.shape[0]
    half, size = depth // 2, pieces[0].shape[0]
    full = weight.shape[1] // 2
    weight[:, :wide] = own_ref[...]
    for core, key, value in ((at_ref[0], got, pieces), (1 - at_ref[0], other, others)):
        before, behind, far_a, far_b = key
        mine = pl.ds(pl.multiple_of(core * half, half), half)
        weight[mine, wide : 2 * wide] = before[:half]
        weight[mine, 3 * wide : full] = behind[:half]
        for rows, src in key_far_rows(core, half, far_a, far_b):
            weight[rows, 2 * wide : 3 * wide] = src[...]
        for rows, src in value_rows(core, at_ref[1], ny, size, value):
            weight[rows, full:] = src[...]
    keep = pltpu.make_async_copy(weight, kept, sem)
    keep.start()
    for d in (1, 3, 0):
        key = dot(feature_ref[...], weight[:, d * wide : (d + 1) * wide])
        value = dot(feature_ref[...], weight[:, full + d * wide : full + (d + 1) * wide])
        if d == 0:
            own_key[...] = key
            own_value[...] = value
        else:
            put_terms(outs[d // 2], slice(None), key, value)
    keep.wait()


def key_far_rows(core, half, far_a, far_b):
    size = half // 2
    for n, src in enumerate((far_a, far_b)):
        yield pl.ds(pl.multiple_of(core * half + n * size, size), size), src


def value_rows(core, at, ny, size, pieces):
    mine, before, behind, far_a, far_b = pieces
    for e, n, src in (
        (0, 0, mine), (1, 0, before), (2, 0, far_a), (2, size // 2, far_b), (3, 0, behind)
    ):
        y = lax.rem(at + ny - e, ny)
        start = pl.multiple_of((core * ny + y) * size + n, size // 2)
        yield pl.ds(start, src.shape[0]), src


def project_far_kernel(ny, at_ref, feature_ref, *refs):
    got, other = refs[:2], refs[2:4]
    pieces, others = refs[4:9], refs[9:14]
    outs, weight = refs[14:16], refs[16]
    wide = got[0].shape[1]
    half, size = weight.shape[0] // 2, pieces[0].shape[0]
    for core, key, value in ((at_ref[0], got, pieces), (1 - at_ref[0], other, others)):
        for rows, src in key_far_rows(core, half, *key):
            weight[rows, :wide] = src[...]
        for rows, src in value_rows(core, at_ref[1], ny, size, value):
            weight[rows, wide:] = src[:, 2 * wide : 3 * wide]
    both = dot(feature_ref[...], weight[...])
    cut = outs[0].shape[0]
    for n, out in enumerate(outs):
        some = slice(n * cut, (n + 1) * cut)
        put_terms(out, slice(None), both[some, :wide], both[some, wide:])


def project_far(where, features, got, other, pieces, others, ny):
    rows, depth = features.shape
    wide = got[0].shape[1]
    return no_grid(
        functools.partial(project_far_kernel, ny),
        "s" + "v" * (1 + 2 * len(got) + 2 * len(pieces)),
        [jax.ShapeDtypeStruct((rows // 2, 3 * wide), BF16)] * 2,
        [pltpu.VMEM((depth, 2 * wide), BF16)],
        4 * rows * depth * wide,
        2 * rows * depth + 4 * depth * wide + 6 * rows * wide,
        "project_far",
        None,
        44,
    )(where, features, *got, *other, *pieces, *others)


def put_terms(ref, rows, key, value):
    wide = key.shape[1]
    high = key.astype(BF16)
    ref[rows, :wide] = high
    ref[rows, wide : 2 * wide] = (key - high.astype(F32)).astype(BF16)
    ref[rows, 2 * wide :] = value.astype(BF16)


def get_terms(ref, rows=slice(None)):
    wide = ref.shape[1] // 3
    term = lambda n: ref[rows, n * wide : (n + 1) * wide].astype(F32)
    return term(0) + term(1), term(2)


def relay_kernel(prev_ref, next_ref, a_ref, b_ref, prev_out, next_out):
    cut = a_ref.shape[0]
    top, bottom = slice(0, cut), slice(cut, None)
    for src, got, out, some, rest in (
        (prev_ref, a_ref, prev_out, top, bottom),
        (next_ref, b_ref, next_out, bottom, top),
    ):
        key, value = get_terms(src, some)
        more_key, more_value = get_terms(got)
        put_terms(out, some, key + more_key, value + more_value)
        out[rest] = src[rest]


def relay(to_prev, to_next, got_a, got_b):
    size = to_prev.size
    return no_grid(
        relay_kernel,
        "vvvv",
        [jax.ShapeDtypeStruct(a.shape, a.dtype) for a in (to_prev, to_next)],
        [],
        10 * size,
        10 * size,
        "relay",
        None,
        57,
    )(to_prev, to_next, got_a, got_b)


def project(where, features, own, got, other, pieces, others, ny):
    rows, depth = features.shape
    wide = own.shape[1]
    full = pieces[0].shape[1]
    weight, own_key, own_value, *sent = no_grid(
        functools.partial(project_kernel, ny),
        "s" + "v" * (2 + 2 * len(got) + 2 * len(pieces)),
        [jax.ShapeDtypeStruct((depth, 2 * full), BF16)]
        + [jax.ShapeDtypeStruct((rows, wide), F32)] * 2
        + [jax.ShapeDtypeStruct((rows, 3 * wide), BF16)] * 2,
        [pltpu.VMEM((depth, 2 * full), BF16), pltpu.SemaphoreType.DMA],
        4 * rows * depth * full,
        2 * rows * depth + 4 * depth * full + 4 * rows * full,
        "project",
        pltpu.HBM,
        57,
    )(where, features, own, *got, *other, *pieces, *others)
    return weight, own_key, own_value, sent


def inverse_of(pre):
    return lax.rsqrt(jnp.mean(pre * pre, axis=-1, keepdims=True) + EPSILON)


def pack_kernel(source_ref, gain_ref, own_key, own_value, *refs):
    parts = refs[:-3]
    pre_ref, out_ref, tiles = refs[-3:]
    per_source, patch = tiles.shape[0] - 1, tiles.shape[1]
    hd = gain_ref.shape[1]
    terms = [get_terms(a) for a in parts]
    pre_ref[...] = sum([a for a, _ in terms], own_key[...])
    value = sum([a for _, a in terms], own_value[...])
    for j in range(pre_ref.shape[1] // hd):
        cols = slice(j * hd, (j + 1) * hd)
        pre = pre_ref[:, cols]
        key = (pre * inverse_of(pre) * gain_ref[...]).astype(BF16).astype(F32)
        low = value[:, cols].astype(BF16).astype(F32)
        both = jnp.concatenate([key, low], axis=1)
        tiles[:per_source, :, 2 * j * hd : 2 * (j + 1) * hd] = both.reshape(
            per_source, patch, 2 * hd
        )
    tiles[per_source] = jnp.zeros(tiles.shape[1:], F32)
    capacity = out_ref.shape[1] // patch

    def fill(s, carry):
        rows = [tiles[source_ref[s * capacity + c]] for c in range(capacity)]
        out_ref[s] = jnp.concatenate(rows, axis=0).astype(BF16)
        return carry

    lax.fori_loop(0, out_ref.shape[0], fill, 0)


def pack(slot_source, gain, own_key, own_value, parts, n_dp, capacity, per_source):
    rows, width = own_key.shape
    patch = rows // per_source
    return no_grid(
        pack_kernel,
        "svvv" + "v" * len(parts),
        [
            jax.ShapeDtypeStruct((rows, width), F32),
            jax.ShapeDtypeStruct((n_dp, capacity * patch, 2 * width), BF16),
        ],
        [pltpu.VMEM((per_source + 1, patch, 2 * width), F32)],
        100 * rows * width,
        40 * rows * width,
        "pack",
        None,
        57,
    )(slot_source, gain, own_key, own_value, *parts)


EXTRA = 16
HD_LANES = 128


def split_rows(total):
    hi = total.astype(BF16).astype(F32)
    mid = (total - hi).astype(BF16).astype(F32)
    low = total - hi - mid
    empty = jnp.zeros((EXTRA - 3, total.shape[1]), F32)
    return jnp.concatenate([hi, mid, low, empty], axis=0).astype(BF16)


def joined_row(rows):
    return jnp.sum(rows.astype(F32), axis=0, keepdims=True)


def unpack_kernel(j, slot_ref, gain_ref, home_ref, pre_ref, out_ref, tiles):
    per_source, patch = tiles.shape[:2]
    rows = per_source * patch
    hd = gain_ref.shape[1]

    def fill(t, carry):
        slot = slot_ref[t]
        pair = home_ref[lax.shift_right_logical(slot, 1)].astype(F32)
        tiles[t] = jnp.where((slot & 1) == 1, pair[patch:], pair[:patch])
        return carry

    lax.fori_loop(0, per_source, fill, 0)
    both = tiles[...].reshape(rows, 2 * hd)
    grad = both[:, :hd]
    pre = pre_ref[:, j * hd : (j + 1) * hd]
    inv = inverse_of(pre)
    terms = jnp.sum(grad * pre * inv, axis=0, keepdims=True)
    scaled = gain_ref[...] * grad
    shared = jnp.mean(scaled * pre, axis=-1, keepdims=True)
    out_ref[:rows, :hd] = (inv * (scaled - pre * inv * inv * shared)).astype(BF16)
    out_ref[:rows, hd:] = both[:, hd:].astype(BF16)
    out_ref[rows:, :hd] = split_rows(terms)
    out_ref[rows:, hd:] = jnp.zeros((EXTRA, hd), BF16)


def unpack(j, send_slot, gain, home, pre):
    rows = pre.shape[0]
    per_source = send_slot.shape[0]
    hd = gain.shape[1]
    return no_grid(
        functools.partial(unpack_kernel, j),
        "svvv",
        [jax.ShapeDtypeStruct((rows + EXTRA, 2 * hd), BF16)],
        [pltpu.VMEM((per_source, rows // per_source, 2 * hd), F32)],
        100 * rows * hd,
        40 * rows * hd,
        "unpack",
    )(send_slot, gain, home, pre)[0]


def weight_grad_kernel(plan, blocks, where_ref, mine_ref, theirs_ref, *refs):
    grads, others = refs[:blocks], refs[blocks : 2 * blocks]
    outs, stage = refs[2 * blocks : -1], refs[-1]
    rows = mine_ref.shape[1]
    wide = grads[0].shape[1]
    hd = wide // 2
    for i in range(blocks):
        total = dot(mine_ref[...], grads[i][:rows]) + dot(theirs_ref[...], others[i][:rows])
        stage[:, :, :, i * wide : (i + 1) * wide] = total.reshape(
            stage.shape[:3] + (wide,)
        ).astype(BF16)
    terms = split_rows(sum(joined_row(a[rows:, :hd]) for a in grads + others))
    first = 0
    for axis, parts, together in plan:
        count = stage.shape[axis]
        if together:
            each = outs[first].shape[0] // count
            mine = [outs[first].at[d * each : (d + 1) * each] for d in range(count)]
            first += 1
        else:
            mine = outs[first : first + count]
            first += count
        size = mine[0].shape[0] - EXTRA
        for d in range(count):
            to = d if together else lax.rem(where_ref[axis] + d, count)
            for i in range(blocks):
                owner = lax.rem(where_ref[2] + blocks - i, blocks)
                for n, part in enumerate(parts):
                    start = pl.multiple_of((n * blocks + owner) * hd, hd)
                    at = slice(i * wide + part * hd, i * wide + (part + 1) * hd)
                    block = stage[to, :, :, at] if axis == 0 else stage[:, to, :, at]
                    mine[d][:size, pl.ds(start, hd)] = block.reshape(size, hd)
            mine[d][size:, :hd] = terms
            mine[d][size:, hd:] = jnp.zeros((EXTRA, mine[d].shape[1] - hd), BF16)


def weight_grad(plan, where, mine, theirs, grads, others, sizes):
    cols, rows = mine.shape
    share = cols // (sizes[0] * sizes[1])
    wide = grads[0].shape[1]
    blocks = len(grads)
    full = blocks * wide
    out = []
    for axis, parts, together in plan:
        count = sizes[axis]
        each, lanes = cols // count + EXTRA, blocks * wide // 2 * len(parts)
        shapes = [(count * each, lanes)] if together else [(each, lanes)] * count
        out += [jax.ShapeDtypeStruct(shape, BF16) for shape in shapes]
    outs = no_grid(
        functools.partial(weight_grad_kernel, plan, blocks),
        "svv" + "v" * (2 * blocks),
        out,
        [pltpu.VMEM((sizes[0], sizes[1], share, full), BF16)],
        10 * rows * cols * full,
        4 * rows * cols + 4 * rows * full + 2 * cols * full,
        "weight_grad",
    )(where, mine, theirs, *grads, *others)
    grouped, first = [], 0
    for axis, _, together in plan:
        n = 1 if together else sizes[axis]
        grouped.append(list(outs[first : first + n]))
        first += n
    return grouped


def middle_kernel(axis, count, each, where_ref, *refs):
    stage = refs[-1]
    outs = refs[-count - 1 : -1]
    hd = HD_LANES
    share = stage.shape[1]
    size = share * count
    for d in range(count):
        outs[d][share:] = jnp.zeros((EXTRA, outs[d].shape[1]), BF16)
    first = at = 0
    for n in each:
        if n == 1:
            span = size + EXTRA
            group = [refs[first].at[i * span : (i + 1) * span] for i in range(refs[first].shape[0] // span)]
        else:
            group = refs[first : first + n]
        first += n
        lanes = slice(at, at + group[0].shape[1])
        total = sum(a[:size].astype(F32) for a in group)
        stage[:, :, lanes] = total.astype(BF16).reshape(count, share, -1)
        terms = split_rows(sum(joined_row(a[size:, :hd]) for a in group))
        for d in range(count):
            outs[d][share:, at : at + hd] = terms
        at = lanes.stop
    for d in range(count):
        outs[d][:share] = stage[lax.rem(where_ref[1 - axis] + d, count)]


def middle(axis, count, where, groups, share):
    cols = sum(group[0].shape[1] for group in groups)
    size = share * count
    flat = [a for group in groups for a in group]
    return list(
        no_grid(
            functools.partial(middle_kernel, axis, count, tuple(len(group) for group in groups)),
            "s" + "v" * len(flat),
            [jax.ShapeDtypeStruct((share + EXTRA, cols), BF16)] * count,
            [pltpu.VMEM((count, share, cols), BF16)],
            20 * size * cols,
            8 * size * cols,
            "middle",
        )(where, *flat)
    )


def last(plans, groups, blocks):
    share = groups[0][0].shape[0] - EXTRA
    hd = HD_LANES
    heads = 1 + max(j for plan in plans for j, _ in plan)
    full = heads * blocks * hd

    def kernel(*refs):
        outs = refs[-3:]
        first = 0
        gain = jnp.zeros((1, hd), F32)
        seen = set()
        for plan, group in zip(plans, groups):
            mine = refs[first : first + len(group)]
            first += len(group)
            total = sum(a[:share].astype(F32) for a in mine)
            at = 0
            for j, parts in plan:
                if j not in seen:
                    seen.add(j)
                    gain = gain + sum(joined_row(a[share:, at : at + hd]) for a in mine)
                for part in parts:
                    for i in range(blocks):
                        to = slice((i * heads + j) * hd, (i * heads + j + 1) * hd)
                        outs[part][:, to] = total[:, at : at + hd]
                        at += hd
        outs[2][...] = gain

    flat = [a for group in groups for a in group]
    grad = jax.ShapeDtypeStruct((share, full), F32)
    return no_grid(
        kernel,
        "v" * len(flat),
        [grad, grad, jax.ShapeDtypeStruct((1, hd), F32)],
        [],
        20 * share * full,
        24 * share * full,
        "last",
    )(*flat)


def feature_grad_kernel(count, *refs):
    grads, weight, out_ref, both = refs[:count], *refs[count:]
    rows = both.shape[0]
    hd = grads[0].shape[1] // 2
    full = count * hd

    @pl.when(pl.program_id(0) == 0)
    def _():
        for i in range(count):
            both[:, i * hd : (i + 1) * hd] = grads[i][:rows, :hd]
            both[:, full + i * hd : full + (i + 1) * hd] = grads[i][:rows, hd:]

    out_ref[...] = dot_nt(both[...], weight[...]).astype(BF16)


def feature_grad(grads, weight, tile):
    rows = grads[0].shape[0] - EXTRA
    depth, full = weight.shape
    whole = pl.BlockSpec(grads[0].shape, lambda i: (0, 0))
    return pl.pallas_call(
        functools.partial(feature_grad_kernel, len(grads)),
        grid=(depth // tile,),
        in_specs=[whole] * len(grads) + [pl.BlockSpec((tile, full), lambda i: (i, 0))],
        out_specs=pl.BlockSpec((rows, tile), lambda i: (0, i)),
        out_shape=jax.ShapeDtypeStruct((rows, depth), BF16),
        scratch_shapes=[pltpu.VMEM((rows, full), BF16)],
        compiler_params=pltpu.CompilerParams(
            dimension_semantics=("arbitrary",), vmem_limit_bytes=WIDE_VMEM_BYTES
        ),
        cost_estimate=pl.CostEstimate(
            flops=4 * rows * depth * full // COST_CUT,
            bytes_accessed=(2 * rows * full + 2 * depth * full + 2 * rows * depth) // COST_CUT,
            transcendentals=0,
        ),
        name="feature_grad",
    )(*grads, weight)


def slot_ranks(readers, sources, per_source):
    by_source = readers.reshape(sources, per_source)
    same_reader = by_source[:, :, None] == by_source[:, None, :]
    positions = jnp.arange(per_source, dtype=jnp.int32)
    before = positions[None, :] < positions[:, None]
    return jnp.sum(jnp.where(same_reader & before[None], 1, 0), axis=2).astype(jnp.int32)


def body(sizes, features, key_weight, value_weight, key_gain, queries, grad_out, tile_dest):
    nx, ny, nc, nz = sizes
    n_dp = nx * ny * nc
    dp, z = lax.axis_index("dp"), lax.axis_index("mp")
    core = lax.rem(dp, nc)
    py = lax.rem(dp // nc, ny)
    px = dp // (nc * ny)
    hd = key_gain.shape[0]
    rows, depth = features.shape
    width = key_weight.shape[1]
    groups = width // hd

    def z_shift(a, d):
        return lax.ppermute(a, "mp", [(i, (i + d) % nz) for i in range(nz)])

    def moved(a, dx, dy, flip=0):
        perm = []
        for i in range(n_dp):
            x, y, c = i // (ny * nc), i // nc % ny, i % nc
            perm.append((i, (((x + dx) % nx) * ny + (y + dy) % ny) * nc + (c ^ flip)))
        return lax.ppermute(a, "dp", perm)

    def swap(a):
        return moved(a, 0, 0, 1)

    x_step = lambda a, d: moved(a, d, 0)
    y_step = lambda a, d: moved(a, 0, d)
    where = jnp.stack([px, py, z])
    core_y = jnp.stack([core, py])

    def piece(weight, d, start, count):
        return lax.dynamic_slice_in_dim(weight, lax.rem(z + d, nz) * depth + start, count)

    half = depth // nc
    share = depth // n_dp
    part = half // ny
    at = core * half + py * part
    value_got = [z_shift(piece(value_weight, d, at, part), d) for d in range(1, nz)]
    by_core = features.T.reshape(nx * ny, nc, share, rows)
    mine = lax.dynamic_index_in_dim(by_core, core, 1, keepdims=False).reshape(-1, rows)
    given = lax.dynamic_index_in_dim(by_core, 1 - core, 1, keepdims=False).reshape(-1, rows)

    def key_piece(d, start, count):
        return piece(key_weight, d, core * half + start, count)

    quarter = half // 2
    to_next = jnp.concatenate([key_piece(1, 0, half), key_piece(2, 0, quarter)], axis=0)
    to_prev = jnp.concatenate([key_piece(nz - 1, 0, half), key_piece(2, quarter, quarter)], axis=0)
    to_next, to_prev, value_got = lax.optimization_barrier((to_next, to_prev, value_got))
    from_prev, from_next = z_shift(to_next, 1), z_shift(to_prev, nz - 1)
    value_y = jnp.concatenate([piece(value_weight, 0, at, part)] + value_got, axis=1)
    before, behind = y_step(value_y, 1), y_step(value_y, ny - 1)
    cut = part // 2
    value_y = [value_y, before, behind, y_step(before[:cut], 1), y_step(behind[cut:], ny - 1)]
    own_key = piece(key_weight, 0, 0, depth)
    from_prev, mine, theirs, own_key = lax.optimization_barrier((from_prev, mine, given, own_key))
    theirs = swap(theirs)
    far_a, far_b = z_shift(from_prev[half:], 1), z_shift(from_next[half:], nz - 1)
    early = [swap(a) for a in value_y[:3]]
    key_got, value_y = lax.optimization_barrier(([from_prev, from_next, far_a, far_b], value_y))
    far_other = [swap(a) for a in key_got[2:]]
    value_other = early + [swap(a) for a in value_y[3:]]
    near, far_other, value_other[3:] = lax.optimization_barrier(
        (key_got[:2], far_other, value_other[3:])
    )
    key_other = [swap(a) for a in near] + far_other
    part_a, part_b = project_far(
        core_y, features, key_got[2:], key_other[2:], value_y, value_other, ny
    )
    got_a, got_b = z_shift(part_a, nz - 1), z_shift(part_b, 1)
    key_got[0] = after(key_got[0], part_a)
    weight_rows, own_key, own_value, (to_prev, to_next) = project(
        core_y, features, own_key, key_got, key_other, value_y, value_other, ny
    )
    got_a, got_b, _ = lax.optimization_barrier((got_a, got_b, to_prev))

    readers = tile_dest[:, 0]
    per_source = readers.shape[0] // n_dp
    patch = rows // per_source
    capacity = max(2, (2 * per_source + n_dp - 1) // n_dp)
    ranks = slot_ranks(readers, n_dp, per_source)
    my_readers = lax.dynamic_slice_in_dim(readers, dp * per_source, per_source)
    my_ranks = lax.dynamic_index_in_dim(ranks, dp, 0, keepdims=False)
    send_slot = my_readers * capacity + my_ranks
    slots = n_dp * capacity
    fills = send_slot[None, :] == jnp.arange(slots, dtype=jnp.int32)[:, None]
    slot_source = jnp.min(
        jnp.where(fills, jnp.arange(per_source, dtype=jnp.int32)[None, :], per_source), axis=1
    )
    counts = jnp.sum(jnp.where(readers.reshape(n_dp, per_source) == dp, 1, 0), axis=1)
    live_slots = jnp.arange(capacity, dtype=jnp.int32)[None, :] < counts[:, None]
    live = jnp.broadcast_to(live_slots[:, :, None], (n_dp, capacity, patch)).reshape(-1)
    bias = jnp.where(
        live[:, None] | (jnp.arange(hd) > 0)[None, :], jnp.float32(0), jnp.float32(-1e30)
    ).astype(BF16)

    to_prev, to_next = relay(to_prev, to_next, got_a, got_b)
    parts = [z_shift(to_prev, nz - 1), z_shift(to_next, 1)]
    gain = key_gain[None]
    key_pre, sent = pack(
        slot_source,
        gain,
        own_key,
        own_value,
        parts,
        n_dp,
        capacity,
        per_source,
    )
    arrived = lax.all_to_all(sent, "dp", split_axis=0, concat_axis=0, tiled=True)
    arrived = arrived.reshape(slots * patch, 2 * width)

    outputs = None
    returned = []
    for j in range(groups):
        *outputs, back = attend(queries, grad_out, arrived, bias, j, groups, hd, outputs)
        returned.append(back.reshape(n_dp, capacity * patch, 2 * hd))

    lengths = (nx, ny)
    steps = (x_step, y_step)
    plans = [[(0, (0, 1), False)], [(1, (0, 1), False)]]
    all_grads, first = [], []
    home = got = None
    for j in range(groups):
        back = returned[j] if home is None else after(returned[j], home)
        home = lax.all_to_all(back, "dp", split_axis=0, concat_axis=0, tiled=True)
        if got is not None:
            home = after(home, *got)
        mine_grads = unpack(j, send_slot, gain, home, key_pre)
        got = [z_shift(mine_grads, d) for d in range(1, nz)]
        if first:
            got, _ = lax.optimization_barrier((got, first[-1]))
        all_grads.append([mine_grads] + got)
        others = [swap(g) for g in all_grads[j]]
        first.append(
            weight_grad(plans[j % 2], where, mine, theirs, all_grads[j], others, lengths)
        )

    def exchange(parts, step):
        return [parts[0]] + [step(parts[d], d) for d in range(1, len(parts))]

    first_y = exchange(first[1][0], y_step)
    late = first[0][0]
    for d in LATE:
        late[d] = after(late[d], first[1][0][0])
    first_x = exchange(late, x_step)

    grads = [g[d] for d in range(nz) for g in all_grads]
    grads[0] = after(grads[0], first[-1][0][0])
    grad_features = feature_grad(grads, weight_rows, 256)

    first_x[1] = after(first_x[1], grad_features)
    first_y[1] = after(first_y[1], grad_features)
    mid_0 = middle(0, ny, where, [first_x], share)
    mid_1 = middle(1, nx, where, [first_y], share)
    grad_key_weight, grad_value_weight, gain_sum = last(
        [[(0, (0, 1))], [(1, (0, 1))]], [exchange(mid_0, y_step), exchange(mid_1, x_step)], nz
    )

    return (
        outputs[0],
        outputs[1],
        grad_features,
        grad_key_weight,
        grad_value_weight,
        gain_sum[0],
    )


def solution(mesh):
    n_dp, nz = mesh.shape["dp"], mesh.shape["mp"]
    nc = 2
    ny = 4
    sizes = (n_dp // (nc * ny), ny, nc, nz)
    in_specs = (P("dp", "mp"), P(None, "mp"), P(None, "mp"), P(), P("dp", "mp"), P("dp", "mp"), P())
    out_specs = (
        P("dp", "mp"),
        P("dp", "mp"),
        P("dp", "mp"),
        P(("mp", "dp"), None),
        P(("mp", "dp"), None),
        P(),
    )
    return jax.shard_map(
        functools.partial(body, sizes),
        mesh=mesh,
        in_specs=in_specs,
        out_specs=out_specs,
        check_vma=False,
    )
```
